32 devices in a mesh: chan: 4 (over z), lag: 8 (over y, x, core).
Axes of the slice: x: 2, y: 2, z: 4, core: 2. Of those that a mesh axis runs over, the one named last changes fastest.
Arguments:
- raw_samples: bfloat16 [8, 512, 800], P(None, 'chan', 'lag'), may hold values from -6 to 6
- decimation_taps: float32 [16], replicated, may hold values from -1.5 to 1.5
- bandpass_taps: float32 [65], replicated, may hold values from -0.75 to 0.75
Outputs:
- correlations: float32 [512, 3, 512, 128], P('chan', None, 'lag')
The draws below stay inside these ranges and needn't reach their ends.
All inputs are finite; a program needn't handle non-finite values.
Results may differ from the reference program's by a relative error of at most 0.0055.
Values may be sent and summed in bfloat16 or wider, within the bound.
No kernel may reach another device: no remote copies, remote signals or barrier semaphores. Data moves between devices by JAX's collectives and lax.ppermute only.
A program may use at most 128 MiB of HBM per device.

```python
import math
import jax
import jax.numpy as jnp
from jax import lax

CH_DEV = 128
WIN = 8
NT = 800
TAPS_DEC = 16
TAPS_BP = 65
NLAG = 512
TD = 400
NCH = 512
NPAIR = 3
N_CHAN = 4


def levels(own_key, extent, shards, low, top_value):
    gain = 1.0
    for axis_at, blocks in shards:
        draws = jax.random.uniform(jax.random.fold_in(jax.random.fold_in(own_key, 6), axis_at), (blocks,), jnp.float32, low / len(shards), top_value / len(shards))
        gain = gain * jnp.repeat(jnp.exp(draws), extent[axis_at] // blocks).reshape((-1,) + (1,) * (len(extent) - 1 - axis_at))
    return gain


def noise(own_key, shape, spread, reach, cuts=(), held_as=jnp.bfloat16):
    result = jax.random.normal(own_key, shape, jnp.float32) * spread
    if len(cuts) > 0:
        result = levels(own_key, shape, cuts, -0.22, 0.18) * result
    return jnp.clip(result, min=-reach, max=reach).astype(held_as)


def setup_inputs(seed: int = 0) -> dict:
    splits = jax.random.split(jax.random.key(seed), 4)
    return {
        "raw_samples": noise(splits[0], (WIN, NCH, NT), 1.0, 6.0, ((1, 4), (2, 8))),
        "decimation_taps": noise(splits[1], (TAPS_DEC,), TAPS_DEC ** -0.5, 1.5, (), jnp.float32),
        "bandpass_taps": noise(splits[2], (TAPS_BP,), TAPS_BP ** -0.5, 0.75, (), jnp.float32),
    }


def reference(raw_samples, decimation_taps, bandpass_taps):
    dec_taps = lax.optimization_barrier(decimation_taps.astype(jnp.bfloat16)).astype(jnp.float32)
    band_taps = lax.optimization_barrier(bandpass_taps.astype(jnp.bfloat16)).astype(jnp.float32)
    samples = raw_samples.astype(jnp.float32)
    dec_count = dec_taps.shape[0]
    padded = jnp.pad(samples, ((0, 0), (0, 0), (dec_count - 1, 0)))
    decimated = jnp.zeros((WIN, NCH, TD), jnp.float32)
    for index in range(dec_count):
        first = dec_count - 1 - index
        decimated = decimated + dec_taps[index] * padded[:, :, first:first + 2 * TD:2]
    decimated = decimated.astype(jnp.bfloat16)
    band_count = band_taps.shape[0]
    dec_padded = jnp.pad(decimated.astype(jnp.float32), ((0, 0), (0, 0), (band_count - 1, 0)))
    filtered = jnp.zeros((WIN, NCH, TD), jnp.float32)
    for index in range(band_count):
        first = band_count - 1 - index
        filtered = filtered + band_taps[index] * dec_padded[:, :, first:first + TD]
    power = lax.optimization_barrier(jnp.mean(filtered * filtered, axis=-1, keepdims=True))
    normalized = (filtered * lax.rsqrt(power + 1e-06)).astype(jnp.bfloat16)
    length = TD + NLAG
    spectra = jnp.fft.rfft(normalized.astype(jnp.float32), n=length, axis=-1)
    blocks = spectra.reshape(WIN, N_CHAN, CH_DEV, spectra.shape[-1])
    factor = 1.0 / math.sqrt(WIN * TD)
    half = NLAG // 2
    stacked = []
    for block in range(N_CHAN):
        rows_out = []
        for distance in range(NPAIR):
            partner = (block + distance) % N_CHAN
            cross = jnp.einsum('wif,wjf->ijf', jnp.conj(blocks[:, block]), blocks[:, partner])
            lagged = jnp.fft.irfft(cross, n=length, axis=-1)
            chosen = jnp.concatenate([lagged[:, :, length - half:], lagged[:, :, :half]], axis=-1)
            rows_out.append(jnp.transpose(chosen, (0, 2, 1)) * factor)
        stacked.append(jnp.stack(rows_out, axis=1))
    return jnp.concatenate(stacked, axis=0).astype(jnp.float32)
```

```python
import functools
import math

import jax
import jax.numpy as jnp
from jax import lax
from jax.experimental import pallas as pl
from jax.experimental.pallas import tpu as pltpu
from jax.sharding import PartitionSpec as P

NLAG = 512
SUB = 8
LANES = 128
F32 = jnp.float32
BF16 = jnp.bfloat16


def ceil_to(value, unit):
    return -(-value // unit) * unit


class Plan:
    def __init__(self, shape, lag_total, dec_taps, bp_taps):
        self.windows, self.channels, self.raw = shape
        self.lag_total = lag_total
        self.dec_taps, self.bp_taps = dec_taps, bp_taps
        self.dec = self.raw // 2
        self.head = dec_taps // 2
        self.whole = self.dec - self.head
        self.edge = dec_taps - 1
        self.rows = ceil_to(self.whole + 2 * self.edge, SUB)
        self.slot = ceil_to(self.rows, 16)
        self.wide = self.windows * self.channels
        self.total = self.dec * lag_total
        self.half = self.total // 2
        self.depth = ceil_to(self.half + SUB, 16)
        self.deep = self.windows * self.depth
        self.lags = NLAG // lag_total
        self.shifts = self.lags // 2 // SUB
        self.held = lag_total * self.slot
        self.joined = self.held + ceil_to(lag_total * self.head, 16)
        self.pad = NLAG // 4
        self.padded = ceil_to(self.pad + self.depth + NLAG // 4, SUB)


def rounded_tap(taps, index):
    return jnp.full((SUB, LANES), taps[index], F32).astype(BF16).astype(F32)[0:1, 0:1]


def local_kernel(plan, taps_ref, raw_ref, out_ref):
    row = lax.broadcasted_iota(jnp.int32, (plan.rows, plan.raw), 0)
    time = lax.broadcasted_iota(jnp.int32, (plan.rows, plan.raw), 1)
    tap = 2 * (row + plan.head) - time
    table = jnp.zeros((plan.rows, plan.raw), F32)
    for k in range(plan.dec_taps):
        table = jnp.where(tap == k, rounded_tap(taps_ref, k), table)
    last = time - (plan.raw - plan.edge) == row - plan.whole
    first = time == row - plan.whole - plan.edge
    is_last = (row >= plan.whole) & (row < plan.whole + plan.edge)
    is_first = (row >= plan.whole + plan.edge) & (row < plan.whole + 2 * plan.edge)
    picked = jnp.where(is_last & last | is_first & first, 1.0, 0.0)
    table = jnp.where(row < plan.whole, table, picked).astype(BF16)
    for w in range(plan.windows):
        out_ref[:, w * plan.channels : (w + 1) * plan.channels] = lax.dot_general(
            table, raw_ref[w], (((1,), (1,)), ((), ())), preferred_element_type=F32
        ).astype(BF16)


def local_rows(plan, raw, taps):
    return pl.pallas_call(
        functools.partial(local_kernel, plan),
        out_shape=jax.ShapeDtypeStruct((plan.rows, plan.wide), BF16),
        in_specs=[pl.BlockSpec(memory_space=pltpu.SMEM), pl.BlockSpec(memory_space=pltpu.VMEM)],
        out_specs=pl.BlockSpec(memory_space=pltpu.VMEM),
    )(taps, raw)


def table_kernel(plan, dec_ref, bp_ref, even_ref, odd_ref, edge_ref):
    span = ceil_to(plan.total + plan.bp_taps, LANES)
    lane = lax.broadcasted_iota(jnp.int32, (1, span), 1)
    base = jnp.zeros((1, span), F32)
    for k in range(plan.bp_taps):
        base = jnp.where(lane == (span - k) % span, rounded_tap(bp_ref, k), base)
    col = lax.broadcasted_iota(jnp.int32, (span, plan.joined), 1)
    time = lax.broadcasted_iota(jnp.int32, (span, plan.joined), 0)
    at = jnp.full((span, plan.joined), -1, jnp.int32)
    for p in range(plan.lag_total):
        start = col - p * plan.slot
        at = jnp.where((start >= 0) & (start < plan.whole), start + p * plan.dec + plan.head, at)
        start = col - plan.held - p * plan.head
        at = jnp.where((start >= 0) & (start < plan.head), start + p * plan.dec, at)
    order = jnp.where(time == at, 1.0, 0.0).astype(BF16)
    for parity, ref in ((0, even_ref), (1, odd_ref)):
        spread = jnp.broadcast_to(base, (plan.half, span))
        taps = pltpu.roll(spread, parity, 1, stride=2, stride_axis=0)
        ref[...] = jnp.dot(taps.astype(BF16), order, preferred_element_type=F32).astype(BF16)
    rows = plan.joined - plan.held
    row = lax.broadcasted_iota(jnp.int32, (rows, plan.held), 0)
    col = lax.broadcasted_iota(jnp.int32, (rows, plan.held), 1)
    tap = jnp.full((rows, plan.held), -1, jnp.int32)
    for p in range(plan.lag_total):
        j = row - p * plan.head
        mine = (j >= 0) & (j < plan.head)
        r = col - p * plan.slot - plan.whole - plan.edge
        tap = jnp.where(mine & (r >= 0) & (r < plan.edge), 2 * j - r, tap)
        r = col - (p - 1) * plan.slot - plan.whole
        tap = jnp.where(mine & (r >= 0) & (r < plan.edge), 2 * j + plan.edge - r, tap)
    table = jnp.zeros((rows, plan.held), F32)
    for k in range(plan.dec_taps):
        table = jnp.where(tap == k, rounded_tap(dec_ref, k), table)
    edge_ref[...] = table.astype(BF16)


def tables(plan, dec_taps, bp_taps):
    smem, vmem = pl.BlockSpec(memory_space=pltpu.SMEM), pl.BlockSpec(memory_space=pltpu.VMEM)
    return pl.pallas_call(
        functools.partial(table_kernel, plan),
        out_shape=(
            jax.ShapeDtypeStruct((plan.half, plan.joined), BF16),
            jax.ShapeDtypeStruct((plan.half, plan.joined), BF16),
            jax.ShapeDtypeStruct((plan.joined - plan.held, plan.held), BF16),
        ),
        in_specs=[smem, smem],
        out_specs=(vmem, vmem, vmem),
        compiler_params=pltpu.CompilerParams(vmem_limit_bytes=32 * 2**20),
        cost_estimate=pl.CostEstimate(flops=500_000_000, bytes_accessed=2_000_000, transcendentals=0),
    )(dec_taps, bp_taps)


def make_series(plan, place_ref, pieces, tables_refs, held, even, odd, ahead, right):
    even_ref, odd_ref, edge_ref = tables_refs
    place = place_ref[0]
    if plan.slot > plan.rows:
        for p in range(plan.lag_total):
            held[(p + 1) * plan.slot - 16 : (p + 1) * plan.slot, :] = jnp.zeros((16, plan.wide), BF16)
    for p, piece in enumerate(pieces):
        at = pl.multiple_of(lax.bitwise_xor(place, p) * plan.slot, 16)
        held[pl.ds(at, plan.rows), :] = piece[...]
    held[plan.held : plan.joined, :] = jnp.dot(
        edge_ref[...], held[0 : plan.held, :], preferred_element_type=F32
    ).astype(BF16)
    for ref in (even, odd, ahead):
        ref[0 : plan.pad, :] = jnp.zeros((plan.pad, plan.wide), F32)
        ref[plan.pad + plan.half - SUB :, :] = jnp.zeros(
            (plan.padded - plan.pad - plan.half + SUB, plan.wide), F32
        )
    step = 2 * LANES
    for c in range(0, plan.wide, step):
        cols = slice(c, c + step)
        block = held[:, cols]
        a = jnp.dot(even_ref[...], block, preferred_element_type=F32)
        b = jnp.dot(odd_ref[...], block, preferred_element_type=F32)
        power = jnp.sum(a * a + b * b, axis=0, keepdims=True) * (1.0 / plan.total)
        scale = lax.rsqrt(power + 1e-06)
        a = (a * scale).astype(BF16).astype(F32)
        b = (b * scale).astype(BF16).astype(F32)
        even[plan.pad : plan.pad + plan.half, cols] = a
        odd[plan.pad : plan.pad + plan.half, cols] = b
        ahead[plan.pad - 1 : plan.pad - 1 + plan.half, cols] = a
    base = place * (plan.lags // 2)
    for w in range(plan.windows):
        cols = slice(w * plan.channels, (w + 1) * plan.channels)
        rows = slice(w * plan.depth, (w + 1) * plan.depth)
        for s in range(plan.shifts):
            at = pl.ds(pl.multiple_of(base + s * SUB, SUB), plan.depth)
            a, b, c = even[at, cols], odd[at, cols], ahead[at, cols]
            to = slice(s * plan.channels, (s + 1) * plan.channels)
            right[0, rows, to] = b.astype(BF16)
            right[1, rows, to] = (a - b).astype(BF16)
            right[2, rows, to] = (c - b).astype(BF16)


def make_left(plan, even, odd, stack, turned):
    for k, ref in enumerate((even, odd)):
        for w in range(plan.windows):
            stack[w * plan.depth : (w + 1) * plan.depth, :] = ref[
                plan.pad : plan.pad + plan.depth, w * plan.channels : (w + 1) * plan.channels
            ]
        turned[k] = stack[...].T


def shift_left(plan, count, turned, left):
    start = pl.program_id(0) * count

    def pair(k, carry):
        parts = []
        for n in range(2):
            i = start + 2 * k + n
            spread = [jnp.broadcast_to(turned[e, pl.ds(i, 1), :], (SUB, plan.deep)) for e in range(2)]
            parts.append([pltpu.roll(x, 0, 1, stride=1, stride_axis=0) for x in spread])
        a = jnp.concatenate([parts[0][0], parts[1][0]], axis=0)
        b = jnp.concatenate([parts[0][1], parts[1][1]], axis=0)
        rows = pl.ds(pl.multiple_of(k * 16, 16), 16)
        left[0, rows, :] = (a + b).astype(BF16)
        left[1, rows, :] = a.astype(BF16)
        left[2, rows, :] = b.astype(BF16)
        return carry

    lax.fori_loop(0, count // 2, pair, 0)


def correlate(plan, count, left, right, out_ref):
    factor = 1.0 / math.sqrt(plan.windows * plan.total)
    step = min(2 * LANES, plan.shifts * plan.channels)
    for c in range(0, plan.shifts * plan.channels, step):
        cols = slice(c, c + step)
        both, even, odd = (
            jnp.dot(left[k], right[k, :, cols], preferred_element_type=F32) for k in range(3)
        )
        for parity, value in ((0, even), (1, odd)):
            value = (both + value) * factor
            for n in range(step // plan.channels):
                s = c // plan.channels + n
                part = value[:, n * plan.channels : (n + 1) * plan.channels]
                out_ref[:, 0, pl.ds(2 * SUB * s + parity, SUB, stride=2), :] = part.reshape(
                    count, SUB, plan.channels
                )


def own_kernel(plan, count, place_ref, *refs):
    n = plan.lag_total
    pieces, tabs, (out_ref, left_ref) = refs[:n], refs[n : n + 3], refs[n + 3 : n + 5]
    held, even, odd, ahead, right, stack, turned = refs[n + 5 :]

    @pl.when(pl.program_id(0) == 0)
    def _():
        make_series(plan, place_ref, pieces, tabs, held, even, odd, ahead, right)
        make_left(plan, even, odd, stack, turned)

    shift_left(plan, count, turned, left_ref)
    correlate(plan, count, left_ref, right, out_ref)


def other_kernel(plan, count, place_ref, *refs):
    n = plan.lag_total
    pieces, tabs, left_ref, out_ref = refs[:n], refs[n : n + 3], refs[n + 3], refs[n + 5]
    held, even, odd, ahead, right = refs[n + 6 :]

    @pl.when(pl.program_id(0) == 0)
    def _():
        make_series(plan, place_ref, pieces, tabs, held, even, odd, ahead, right)

    correlate(plan, count, left_ref, right, out_ref)


def block_call(plan, count, pairs, distance, place, pieces, tabs, left=None, out=None):
    whole = lambda shape: pl.BlockSpec(shape, lambda i: (0,) * len(shape))
    out_shape = jax.ShapeDtypeStruct((plan.channels, pairs, plan.lags, plan.channels), F32)
    left_shape = jax.ShapeDtypeStruct((3, plan.channels * SUB, plan.deep), BF16)
    out_spec = pl.BlockSpec((count, 1, plan.lags, plan.channels), lambda i: (i, distance, 0, 0))
    left_spec = pl.BlockSpec((3, count * SUB, plan.deep), lambda i: (0, i, 0))
    vmem = pl.BlockSpec(memory_space=pltpu.VMEM)
    in_specs = [pl.BlockSpec(memory_space=pltpu.SMEM)] + [vmem] * (plan.lag_total + 3)
    scratch = [
        pltpu.VMEM((plan.joined, plan.wide), BF16),
        pltpu.VMEM((plan.padded, plan.wide), F32),
        pltpu.VMEM((plan.padded, plan.wide), F32),
        pltpu.VMEM((plan.padded, plan.wide), F32),
        pltpu.VMEM((3, plan.deep, plan.shifts * plan.channels), BF16),
    ]
    flops = 2 * 3 * plan.channels * SUB * plan.deep * plan.shifts * plan.channels
    cost = pl.CostEstimate(flops=flops, bytes_accessed=16 * 2**20, transcendentals=0)
    params = pltpu.CompilerParams(vmem_limit_bytes=48 * 2**20)
    if left is None:
        return pl.pallas_call(
            functools.partial(own_kernel, plan, count),
            grid=(plan.channels // count,),
            out_shape=(out_shape, left_shape),
            in_specs=in_specs,
            out_specs=(out_spec, left_spec),
            scratch_shapes=scratch
            + [pltpu.VMEM((plan.deep, plan.channels), F32), pltpu.VMEM((2, plan.channels, plan.deep), F32)],
            compiler_params=params,
            cost_estimate=cost,
            name="own_block",
        )(place, *pieces, *tabs)
    return pl.pallas_call(
        functools.partial(other_kernel, plan, count),
        grid=(plan.channels // count,),
        out_shape=out_shape,
        in_specs=in_specs + [left_spec, pl.BlockSpec(memory_space=pl.ANY)],
        out_specs=out_spec,
        scratch_shapes=scratch,
        input_output_aliases={len(in_specs) + 1: 0},
        compiler_params=params,
        cost_estimate=cost,
        name="other_block",
    )(place, *pieces, *tabs, left, out)


def swap(piece, mask):
    count = lax.axis_size("lag")
    return lax.ppermute(piece, "lag", [(i ^ mask, i) for i in range(count)])


def from_ahead(piece, distance):
    count = lax.axis_size("chan")
    return lax.ppermute(piece, "chan", [((i + distance) % count, i) for i in range(count)])


def gather_pieces(piece):
    count = lax.axis_size("lag")
    mine = {0: piece}
    for mask in range(2, count, 2):
        mine[mask] = swap(piece, mask)
    for mask in range(0, count, 2):
        mine[mask + 1] = swap(mine[mask], 1)
    return [mine[p] for p in range(count)]


def shards(raw_samples, decimation_taps, bandpass_taps):
    plan = Plan(raw_samples.shape, lax.axis_size("lag"), decimation_taps.shape[0], bandpass_taps.shape[0])
    pairs = lax.axis_size("chan") // 2 + 1
    place = lax.axis_index("lag").astype(jnp.int32).reshape(1)
    piece = local_rows(plan, raw_samples, decimation_taps)
    tabs = tables(plan, decimation_taps, bandpass_taps)
    count = 32
    out, left = block_call(plan, count, pairs, 0, place, gather_pieces(piece), tabs)
    for distance in range(1, pairs):
        pieces = gather_pieces(from_ahead(piece, distance))
        out = block_call(plan, count, pairs, distance, place, pieces, tabs, left, out)
    return out


def solution(mesh):
    placed = (P(None, "chan", "lag"), P(), P())
    return jax.shard_map(
        shards, mesh=mesh, in_specs=placed, out_specs=P("chan", None, "lag", None), check_vma=False
    )
```

```python
import functools
import math

import jax
import jax.numpy as jnp
from jax import lax
from jax.experimental import pallas as pl
from jax.experimental.pallas import tpu as pltpu
from jax.sharding import PartitionSpec as P

NLAG = 512
SUB = 8
LANES = 128
F32 = jnp.float32
BF16 = jnp.bfloat16
SMEM = pl.BlockSpec(memory_space=pltpu.SMEM)
VMEM = pl.BlockSpec(memory_space=pltpu.VMEM)


def ceil_to(value, unit):
    return -(-value // unit) * unit


class Plan:
    def __init__(self, shape, lag_total, dec_taps, bp_taps):
        self.windows, self.channels, self.raw = shape
        self.lag_total = lag_total
        self.dec_taps, self.bp_taps = dec_taps, bp_taps
        self.dec = self.raw // 2
        self.head = dec_taps // 2
        self.whole = self.dec - self.head
        self.edge = dec_taps - 1
        self.rows = ceil_to(self.whole + 2 * self.edge, SUB)
        self.slot = ceil_to(self.rows, 16)
        self.wide = self.windows * self.channels
        self.total = self.dec * lag_total
        self.half = self.total // 2
        self.depth = ceil_to(self.half + SUB, 16)
        self.deep = self.windows * self.depth
        self.lags = NLAG // lag_total
        self.shifts = self.lags // 2 // SUB
        self.held = lag_total * self.slot
        self.joined = self.held + ceil_to(lag_total * self.head, 16)
        self.pad = NLAG // 4
        self.padded = ceil_to(self.pad + self.depth + NLAG // 4, SUB)


def rounded_tap(taps, index):
    return taps[0:1, index : index + 1].astype(BF16).astype(F32)


def local_kernel(plan, taps_ref, raw_ref, out_ref, spread):
    row = lax.broadcasted_iota(jnp.int32, (plan.rows, plan.raw), 0)
    time = lax.broadcasted_iota(jnp.int32, (plan.rows, plan.raw), 1)
    tap = 2 * (row + plan.head) - time
    table = jnp.zeros((plan.rows, plan.raw), F32)
    for k in range(plan.dec_taps):
        table = jnp.where(tap == k, rounded_tap(taps_ref, k), table)
    last = time - (plan.raw - plan.edge) == row - plan.whole
    first = time == row - plan.whole - plan.edge
    is_last = (row >= plan.whole) & (row < plan.whole + plan.edge)
    is_first = (row >= plan.whole + plan.edge) & (row < plan.whole + 2 * plan.edge)
    picked = jnp.where(is_last & last | is_first & first, 1.0, 0.0)
    table = jnp.where(row < plan.whole, table, picked).astype(BF16)
    spread[...] = raw_ref[...].astype(F32).reshape(plan.raw * plan.windows, plan.channels)
    for w in range(plan.windows):
        series = spread[pl.ds(w, plan.raw, stride=plan.windows), :].astype(BF16)
        out_ref[:, w * plan.channels : (w + 1) * plan.channels] = jnp.dot(
            table, series, preferred_element_type=F32
        ).astype(BF16)


def local_rows(plan, raw, taps):
    return pl.pallas_call(
        functools.partial(local_kernel, plan),
        out_shape=jax.ShapeDtypeStruct((plan.rows, plan.wide), BF16),
        in_specs=[VMEM, VMEM],
        out_specs=VMEM,
        scratch_shapes=[pltpu.VMEM((plan.raw * plan.windows, plan.channels), F32)],
        name="local_rows",
    )(taps, jnp.transpose(raw, (2, 0, 1)))


def table_kernel(plan, dec_ref, bp_ref, even_ref, odd_ref, edge_ref):
    span = ceil_to(plan.total + plan.bp_taps, LANES)
    lane = lax.broadcasted_iota(jnp.int32, (1, span), 1)
    base = jnp.zeros((1, span), F32)
    for k in range(plan.bp_taps):
        base = jnp.where(lane == (span - k) % span, rounded_tap(bp_ref, k), base)
    col = lax.broadcasted_iota(jnp.int32, (span, plan.joined), 1)
    time = lax.broadcasted_iota(jnp.int32, (span, plan.joined), 0)
    at = jnp.full((span, plan.joined), -1, jnp.int32)
    for p in range(plan.lag_total):
        start = col - p * plan.slot
        at = jnp.where((start >= 0) & (start < plan.whole), start + p * plan.dec + plan.head, at)
        start = col - plan.held - p * plan.head
        at = jnp.where((start >= 0) & (start < plan.head), start + p * plan.dec, at)
    order = jnp.where(time == at, 1.0, 0.0).astype(BF16)
    for parity, ref in ((0, even_ref), (1, odd_ref)):
        spread = jnp.broadcast_to(base, (plan.half, span))
        taps = pltpu.roll(spread, parity, 1, stride=2, stride_axis=0)
        ref[...] = jnp.dot(taps.astype(BF16), order, preferred_element_type=F32).astype(BF16)
    rows = plan.joined - plan.held
    row = lax.broadcasted_iota(jnp.int32, (rows, plan.held), 0)
    col = lax.broadcasted_iota(jnp.int32, (rows, plan.held), 1)
    tap = jnp.full((rows, plan.held), -1, jnp.int32)
    for p in range(plan.lag_total):
        j = row - p * plan.head
        mine = (j >= 0) & (j < plan.head)
        r = col - p * plan.slot - plan.whole - plan.edge
        tap = jnp.where(mine & (r >= 0) & (r < plan.edge), 2 * j - r, tap)
        r = col - (p - 1) * plan.slot - plan.whole
        tap = jnp.where(mine & (r >= 0) & (r < plan.edge), 2 * j + plan.edge - r, tap)
    table = jnp.zeros((rows, plan.held), F32)
    for k in range(plan.dec_taps):
        table = jnp.where(tap == k, rounded_tap(dec_ref, k), table)
    edge_ref[...] = table.astype(BF16)


def tables(plan, dec_taps, bp_taps):
    return pl.pallas_call(
        functools.partial(table_kernel, plan),
        out_shape=(
            jax.ShapeDtypeStruct((plan.half, plan.joined), BF16),
            jax.ShapeDtypeStruct((plan.half, plan.joined), BF16),
            jax.ShapeDtypeStruct((plan.joined - plan.held, plan.held), BF16),
        ),
        in_specs=[VMEM, VMEM],
        out_specs=(VMEM, VMEM, VMEM),
        compiler_params=pltpu.CompilerParams(vmem_limit_bytes=20 * 2**20),
        cost_estimate=pl.CostEstimate(flops=500_000_000, bytes_accessed=2_000_000, transcendentals=0),
        name="tables",
    )(dec_taps, bp_taps)


def make_series(plan, place_ref, pieces, tables_refs, held, even, odd, ahead, right):
    place = place_ref[0]
    if plan.slot > plan.rows:
        for p in range(plan.lag_total):
            held[(p + 1) * plan.slot - 16 : (p + 1) * plan.slot, :] = jnp.zeros((16, plan.wide), BF16)
    for p in range(plan.lag_total):
        at = pl.multiple_of(lax.bitwise_xor(place, p) * plan.slot, 16)
        held[pl.ds(at, plan.rows), :] = pieces[p][...]
    filter_block(plan, tables_refs, held, even, odd, ahead)
    lay_right(plan, place, even, odd, ahead, right)


def filter_block(plan, tables_refs, held, even, odd, ahead):
    even_ref, odd_ref, edge_ref = tables_refs
    held[plan.held : plan.joined, :] = jnp.dot(
        edge_ref[...], held[0 : plan.held, :], preferred_element_type=F32
    ).astype(BF16)
    for ref in (even, odd, ahead):
        ref[0 : plan.pad, :] = jnp.zeros((plan.pad, plan.wide), F32)
        ref[plan.pad + plan.half - SUB :, :] = jnp.zeros(
            (plan.padded - plan.pad - plan.half + SUB, plan.wide), F32
        )
    step = 2 * LANES
    for c in range(0, plan.wide, step):
        cols = slice(c, c + step)
        block = held[:, cols]
        a = jnp.dot(even_ref[...], block, preferred_element_type=F32)
        b = jnp.dot(odd_ref[...], block, preferred_element_type=F32)
        power = jnp.sum(a * a + b * b, axis=0, keepdims=True) * (1.0 / plan.total)
        scale = lax.rsqrt(power + 1e-06)
        a = (a * scale).astype(BF16).astype(F32)
        b = (b * scale).astype(BF16).astype(F32)
        even[plan.pad : plan.pad + plan.half, cols] = a
        odd[plan.pad : plan.pad + plan.half, cols] = b
        ahead[plan.pad - 1 : plan.pad - 1 + plan.half, cols] = a


def lay_right(plan, place, even, odd, ahead, right):
    base = place * (plan.lags // 2)
    for w in range(plan.windows):
        cols = slice(w * plan.channels, (w + 1) * plan.channels)
        rows = slice(w * plan.depth, (w + 1) * plan.depth)
        for s in range(plan.shifts):
            at = pl.ds(pl.multiple_of(base + s * SUB, SUB), plan.depth)
            a, b, c = even[at, cols], odd[at, cols], ahead[at, cols]
            to = slice(s * plan.channels, (s + 1) * plan.channels)
            right[0, rows, to] = b.astype(BF16)
            right[1, rows, to] = (a - b).astype(BF16)
            right[2, rows, to] = (c - b).astype(BF16)


def make_left(plan, even, odd, stacks, mixes, left):
    for ref, stack in zip((even, odd), stacks, strict=True):
        stack[0:SUB, :] = jnp.zeros((SUB, plan.channels), F32)
        for w in range(plan.windows):
            stack[SUB + w * plan.depth : SUB + (w + 1) * plan.depth, :] = ref[
                plan.pad : plan.pad + plan.depth, w * plan.channels : (w + 1) * plan.channels
            ]
    for n, c in enumerate(range(0, plan.deep, LANES)):
        mixed = mixes[n % 2]
        for delay in range(SUB):
            rows = slice(SUB - delay + c, SUB - delay + c + LANES)
            for e, stack in enumerate(stacks):
                mixed[e, pl.ds(delay, plan.channels, stride=SUB), :] = stack[rows, :].T
        for r in range(0, plan.channels * SUB, LANES):
            a, b = (mixed[e, r : r + LANES, :] for e in range(2))
            for k, value in enumerate((a + b, a, b)):
                left[k, r : r + LANES, c : c + LANES] = value.astype(BF16)


def correlate(plan, count, left, right, out_ref):
    factor = 1.0 / math.sqrt(plan.windows * plan.total)
    step = min(2 * LANES, plan.shifts * plan.channels)
    for c in range(0, plan.shifts * plan.channels, step):
        cols = slice(c, c + step)
        rows = pl.ds(pl.multiple_of(pl.program_id(0) * count * SUB, count * SUB), count * SUB)
        both, even, odd = (
            jnp.dot(left[k, rows, :], right[k, :, cols], preferred_element_type=F32) for k in range(3)
        )
        for parity, value in ((0, even), (1, odd)):
            value = (both + value) * factor
            for n in range(step // plan.channels):
                s = c // plan.channels + n
                part = value[:, n * plan.channels : (n + 1) * plan.channels]
                out_ref[:, 0, pl.ds(2 * SUB * s + parity, SUB, stride=2), :] = part.reshape(
                    count, SUB, plan.channels
                )


def own_kernel(plan, place_ref, *refs):
    n = plan.lag_total
    pieces, tabs, (left_ref, right_ref) = refs[:n], refs[n : n + 3], refs[n + 3 : n + 5]
    held, even, odd, ahead, *rest = refs[n + 5 :]
    make_series(plan, place_ref, pieces, tabs, held, even, odd, ahead, right_ref)
    make_left(plan, even, odd, rest[:2], rest[2:], left_ref)


def first_kernel(plan, count, left_ref, right_ref, out_ref):
    correlate(plan, count, left_ref, right_ref, out_ref)


def other_kernel(plan, count, place_ref, *refs):
    n = plan.lag_total
    pieces, tabs, left_ref, out_ref = refs[:n], refs[n : n + 3], refs[n + 3], refs[n + 5]
    held, even, odd, ahead, right = refs[n + 6 :]

    @pl.when(pl.program_id(0) == 0)
    def _():
        make_series(plan, place_ref, pieces, tabs, held, even, odd, ahead, right)

    correlate(plan, count, left_ref, right, out_ref)


def series_scratch(plan):
    return [pltpu.VMEM((plan.joined, plan.wide), BF16)] + [pltpu.VMEM((plan.padded, plan.wide), F32)] * 3


def prepare_own(plan, place, pieces, tabs):
    return pl.pallas_call(
        functools.partial(own_kernel, plan),
        out_shape=(
            jax.ShapeDtypeStruct((3, plan.channels * SUB, plan.deep), BF16),
            jax.ShapeDtypeStruct((3, plan.deep, plan.shifts * plan.channels), BF16),
        ),
        in_specs=[SMEM] + [VMEM] * (plan.lag_total + 3),
        out_specs=(VMEM, VMEM),
        scratch_shapes=series_scratch(plan)
        + [pltpu.VMEM((SUB + plan.deep, plan.channels), F32)] * 2
        + [pltpu.VMEM((2, plan.channels * SUB, LANES), F32)] * 2,
        compiler_params=pltpu.CompilerParams(vmem_limit_bytes=33 * 2**20),
        cost_estimate=pl.CostEstimate(flops=5_000_000_000, bytes_accessed=2**20, transcendentals=0),
        name="prepare_own",
    )(place, *pieces, *tabs)


def correlation_parts(plan, count, pairs, distance):
    out_shape = jax.ShapeDtypeStruct((plan.channels, pairs, plan.lags, plan.channels), F32)
    out_spec = pl.BlockSpec((count, 1, plan.lags, plan.channels), lambda i: (i, distance, 0, 0))
    flops = 2 * 3 * plan.channels * SUB * plan.deep * plan.shifts * plan.channels
    cost = pl.CostEstimate(flops=flops, bytes_accessed=8 * 2**20, transcendentals=0)
    return out_shape, out_spec, cost


def own_correlation(plan, count, pairs, left, right):
    out_shape, out_spec, cost = correlation_parts(plan, count, pairs, 0)
    return pl.pallas_call(
        functools.partial(first_kernel, plan, count),
        grid=(plan.channels // count,),
        out_shape=out_shape,
        in_specs=[VMEM, VMEM],
        out_specs=out_spec,
        compiler_params=pltpu.CompilerParams(vmem_limit_bytes=24 * 2**20),
        cost_estimate=cost,
        name="own_correlation",
    )(left, right)


def other_correlation(plan, count, pairs, distance, place, pieces, tabs, left, out):
    out_shape, out_spec, cost = correlation_parts(plan, count, pairs, distance)
    in_specs = [SMEM] + [VMEM] * (plan.lag_total + 4) + [pl.BlockSpec(memory_space=pl.ANY)]
    return pl.pallas_call(
        functools.partial(other_kernel, plan, count),
        grid=(plan.channels // count,),
        out_shape=out_shape,
        in_specs=in_specs,
        out_specs=out_spec,
        scratch_shapes=series_scratch(plan)
        + [pltpu.VMEM((3, plan.deep, plan.shifts * plan.channels), BF16)],
        input_output_aliases={len(in_specs) - 1: 0},
        compiler_params=pltpu.CompilerParams(vmem_limit_bytes=30 * 2**20),
        cost_estimate=cost,
        name="other_correlation",
    )(place, *pieces, *tabs, left, out)


def swap(piece, mask):
    count = lax.axis_size("lag")
    return lax.ppermute(piece, "lag", [(i ^ mask, i) for i in range(count)])


def from_ahead(piece, distance):
    count = lax.axis_size("chan")
    return lax.ppermute(piece, "chan", [((i + distance) % count, i) for i in range(count)])


def same_core(piece):
    return [swap(piece, mask) if mask else piece for mask in range(0, lax.axis_size("lag"), 2)]


def both_cores(held):
    return [x for piece in held for x in (piece, swap(piece, 1))]


def shards(raw_samples, decimation_taps, bandpass_taps):
    plan = Plan(raw_samples.shape, lax.axis_size("lag"), decimation_taps.shape[0], bandpass_taps.shape[0])
    pairs = lax.axis_size("chan") // 2 + 1
    place = lax.axis_index("lag").astype(jnp.int32).reshape(1)
    dec_taps = decimation_taps.reshape(1, -1)
    piece = local_rows(plan, raw_samples, dec_taps)
    tabs = tables(plan, dec_taps, bandpass_taps.reshape(1, -1))
    count = 32
    held = same_core(piece)
    tabs, held[1:] = lax.optimization_barrier((tabs, held[1:]))
    left, right = prepare_own(plan, place, both_cores(held), tabs)
    ahead = [from_ahead(x, 1) for x in held]
    left, ahead = lax.optimization_barrier((left, ahead))
    out = own_correlation(plan, count, pairs, left, right)
    for distance in range(1, pairs):
        pieces = both_cores(ahead)
        if distance + 1 < pairs:
            ahead = [from_ahead(x, 1) for x in ahead]
        out_next = other_correlation(plan, count, pairs, distance, place, pieces, tabs, left, out)
        if distance + 1 < pairs:
            out_next, ahead = lax.optimization_barrier((out_next, ahead))
        out = out_next
    return out


def solution(mesh):
    placed = (P(None, "chan", "lag"), P(), P())
    return jax.shard_map(
        shards, mesh=mesh, in_specs=placed, out_specs=P("chan", None, "lag", None), check_vma=False
    )
```

```python
import functools
import math

import jax
import jax.numpy as jnp
from jax import lax
from jax.experimental import pallas as pl
from jax.experimental.pallas import tpu as pltpu
from jax.sharding import PartitionSpec as P

NLAG = 512
SUB = 8
LANES = 128
F32 = jnp.float32
BF16 = jnp.bfloat16
SMEM = pl.BlockSpec(memory_space=pltpu.SMEM)
VMEM = pl.BlockSpec(memory_space=pltpu.VMEM)


def ceil_to(value, unit):
    return -(-value // unit) * unit


class Plan:
    def __init__(self, shape, lag_total, dec_taps, bp_taps):
        self.windows, self.channels, self.raw = shape
        self.lag_total = lag_total
        self.dec_taps, self.bp_taps = dec_taps, bp_taps
        self.dec = self.raw // 2
        self.head = dec_taps // 2
        self.whole = self.dec - self.head
        self.edge = dec_taps - 1
        self.rows = ceil_to(self.whole + 2 * self.edge, SUB)
        self.slot = ceil_to(self.rows, 16)
        self.wide = self.windows * self.channels
        self.total = self.dec * lag_total
        self.half = self.total // 2
        self.depth = ceil_to(self.half + SUB, 16)
        self.deep = self.windows * self.depth
        self.lags = NLAG // lag_total
        self.shifts = self.lags // 2 // SUB
        self.held = lag_total * self.slot
        self.joined = self.held + ceil_to(lag_total * self.head, 16)
        self.pad = NLAG // 4
        self.padded = ceil_to(self.pad + self.depth + NLAG // 4, SUB)


def rounded_tap(taps, index):
    return taps[0:1, index : index + 1].astype(BF16).astype(F32)


def local_kernel(plan, taps_ref, raw_ref, sent_ref, kept_ref, spread):
    row = lax.broadcasted_iota(jnp.int32, (plan.rows, plan.raw), 0)
    time = lax.broadcasted_iota(jnp.int32, (plan.rows, plan.raw), 1)
    tap = 2 * (row + plan.head) - time
    table = jnp.zeros((plan.rows, plan.raw), F32)
    for k in range(plan.dec_taps):
        table = jnp.where(tap == k, rounded_tap(taps_ref, k), table)
    last = time - (plan.raw - plan.edge) == row - plan.whole
    first = time == row - plan.whole - plan.edge
    is_last = (row >= plan.whole) & (row < plan.whole + plan.edge)
    is_first = (row >= plan.whole + plan.edge) & (row < plan.whole + 2 * plan.edge)
    picked = jnp.where(is_last & last | is_first & first, 1.0, 0.0)
    table = jnp.where(row < plan.whole, table, picked).astype(BF16)
    spread[...] = raw_ref[...].astype(F32).reshape(plan.raw * plan.windows, plan.channels)
    for w in range(plan.windows):
        series = spread[pl.ds(w, plan.raw, stride=plan.windows), :].astype(BF16)
        rows = jnp.dot(table, series, preferred_element_type=F32).astype(BF16)
        for ref in (sent_ref, kept_ref):
            ref[:, w * plan.channels : (w + 1) * plan.channels] = rows


def local_rows(plan, raw, taps):
    return pl.pallas_call(
        functools.partial(local_kernel, plan),
        out_shape=[jax.ShapeDtypeStruct((plan.rows, plan.wide), BF16)] * 2,
        in_specs=[VMEM, VMEM],
        out_specs=[VMEM, VMEM],
        scratch_shapes=[pltpu.VMEM((plan.raw * plan.windows, plan.channels), F32)],
        name="local_rows",
    )(taps, jnp.transpose(raw, (2, 0, 1)))


def table_kernel(plan, dec_ref, bp_ref, even_ref, odd_ref, edge_ref):
    span = ceil_to(plan.total + plan.bp_taps, LANES)
    lane = lax.broadcasted_iota(jnp.int32, (1, span), 1)
    base = jnp.zeros((1, span), F32)
    for k in range(plan.bp_taps):
        base = jnp.where(lane == (span - k) % span, rounded_tap(bp_ref, k), base)
    col = lax.broadcasted_iota(jnp.int32, (span, plan.joined), 1)
    time = lax.broadcasted_iota(jnp.int32, (span, plan.joined), 0)
    at = jnp.full((span, plan.joined), -1, jnp.int32)
    for p in range(plan.lag_total):
        start = col - p * plan.slot
        at = jnp.where((start >= 0) & (start < plan.whole), start + p * plan.dec + plan.head, at)
        start = col - plan.held - p * plan.head
        at = jnp.where((start >= 0) & (start < plan.head), start + p * plan.dec, at)
    order = jnp.where(time == at, 1.0, 0.0).astype(BF16)
    for parity, ref in ((0, even_ref), (1, odd_ref)):
        spread = jnp.broadcast_to(base, (plan.half, span))
        taps = pltpu.roll(spread, parity, 1, stride=2, stride_axis=0)
        ref[...] = jnp.dot(taps.astype(BF16), order, preferred_element_type=F32).astype(BF16)
    rows = plan.joined - plan.held
    row = lax.broadcasted_iota(jnp.int32, (rows, plan.held), 0)
    col = lax.broadcasted_iota(jnp.int32, (rows, plan.held), 1)
    tap = jnp.full((rows, plan.held), -1, jnp.int32)
    for p in range(plan.lag_total):
        j = row - p * plan.head
        mine = (j >= 0) & (j < plan.head)
        r = col - p * plan.slot - plan.whole - plan.edge
        tap = jnp.where(mine & (r >= 0) & (r < plan.edge), 2 * j - r, tap)
        r = col - (p - 1) * plan.slot - plan.whole
        tap = jnp.where(mine & (r >= 0) & (r < plan.edge), 2 * j + plan.edge - r, tap)
    table = jnp.zeros((rows, plan.held), F32)
    for k in range(plan.dec_taps):
        table = jnp.where(tap == k, rounded_tap(dec_ref, k), table)
    edge_ref[...] = table.astype(BF16)


def tables(plan, dec_taps, bp_taps):
    return pl.pallas_call(
        functools.partial(table_kernel, plan),
        out_shape=(
            jax.ShapeDtypeStruct((plan.half, plan.joined), BF16),
            jax.ShapeDtypeStruct((plan.half, plan.joined), BF16),
            jax.ShapeDtypeStruct((plan.joined - plan.held, plan.held), BF16),
        ),
        in_specs=[VMEM, VMEM],
        out_specs=(VMEM, VMEM, VMEM),
        compiler_params=pltpu.CompilerParams(vmem_limit_bytes=20 * 2**20),
        cost_estimate=pl.CostEstimate(flops=500_000_000, bytes_accessed=2_000_000, transcendentals=0),
        name="tables",
    )(dec_taps, bp_taps)


def make_series(plan, place_ref, pieces, tables_refs, held, even, odd, ahead, right):
    place = place_ref[0]
    if plan.slot > plan.rows:
        for p in range(plan.lag_total):
            held[(p + 1) * plan.slot - 16 : (p + 1) * plan.slot, :] = jnp.zeros((16, plan.wide), BF16)
    for p in range(plan.lag_total):
        at = pl.multiple_of(lax.bitwise_xor(place, p) * plan.slot, 16)
        held[pl.ds(at, plan.rows), :] = pieces[p][...]
    filter_block(plan, tables_refs, held, even, odd, ahead)
    lay_right(plan, place, even, odd, ahead, right)


def filter_block(plan, tables_refs, held, even, odd, ahead):
    even_ref, odd_ref, edge_ref = tables_refs
    held[plan.held : plan.joined, :] = jnp.dot(
        edge_ref[...], held[0 : plan.held, :], preferred_element_type=F32
    ).astype(BF16)
    for ref in (even, odd, ahead):
        ref[0 : plan.pad, :] = jnp.zeros((plan.pad, plan.wide), F32)
        ref[plan.pad + plan.half - SUB :, :] = jnp.zeros(
            (plan.padded - plan.pad - plan.half + SUB, plan.wide), F32
        )
    step = 2 * LANES
    for c in range(0, plan.wide, step):
        cols = slice(c, c + step)
        block = held[:, cols]
        a = jnp.dot(even_ref[...], block, preferred_element_type=F32)
        b = jnp.dot(odd_ref[...], block, preferred_element_type=F32)
        power = jnp.sum(a * a + b * b, axis=0, keepdims=True) * (1.0 / plan.total)
        scale = lax.rsqrt(power + 1e-06)
        a = (a * scale).astype(BF16).astype(F32)
        b = (b * scale).astype(BF16).astype(F32)
        even[plan.pad : plan.pad + plan.half, cols] = a
        odd[plan.pad : plan.pad + plan.half, cols] = b
        ahead[plan.pad - 1 : plan.pad - 1 + plan.half, cols] = a


def lay_right(plan, place, even, odd, ahead, right):
    base = place * (plan.lags // 2)
    for w in range(plan.windows):
        cols = slice(w * plan.channels, (w + 1) * plan.channels)
        rows = slice(w * plan.depth, (w + 1) * plan.depth)
        for s in range(plan.shifts):
            at = pl.ds(pl.multiple_of(base + s * SUB, SUB), plan.depth)
            a, b, c = even[at, cols], odd[at, cols], ahead[at, cols]
            to = slice(s * plan.channels, (s + 1) * plan.channels)
            right[0, rows, to] = b.astype(BF16)
            right[1, rows, to] = (a - b).astype(BF16)
            right[2, rows, to] = (c - b).astype(BF16)


def make_left(plan, even, odd, stacks, mixes, left):
    for ref, stack in zip((even, odd), stacks, strict=True):
        stack[0:SUB, :] = jnp.zeros((SUB, plan.channels), F32)
        for w in range(plan.windows):
            stack[SUB + w * plan.depth : SUB + (w + 1) * plan.depth, :] = ref[
                plan.pad : plan.pad + plan.depth, w * plan.channels : (w + 1) * plan.channels
            ]
    for n, c in enumerate(range(0, plan.deep, LANES)):
        mixed = mixes[n % 2]
        for delay in range(SUB):
            rows = slice(SUB - delay + c, SUB - delay + c + LANES)
            for e, stack in enumerate(stacks):
                mixed[e, pl.ds(delay, plan.channels, stride=SUB), :] = stack[rows, :].T
        for r in range(0, plan.channels * SUB, LANES):
            a, b = (mixed[e, r : r + LANES, :] for e in range(2))
            for k, value in enumerate((a + b, a, b)):
                left[k, r : r + LANES, c : c + LANES] = value.astype(BF16)


def correlate(plan, count, left, right, out_ref):
    factor = 1.0 / math.sqrt(plan.windows * plan.total)
    step = min(2 * LANES, plan.shifts * plan.channels)
    for c in range(0, plan.shifts * plan.channels, step):
        cols = slice(c, c + step)
        rows = pl.ds(pl.multiple_of(pl.program_id(0) * count * SUB, count * SUB), count * SUB)
        both, even, odd = (
            jnp.dot(left[k, rows, :], right[k, :, cols], preferred_element_type=F32) for k in range(3)
        )
        for parity, value in ((0, even), (1, odd)):
            value = (both + value) * factor
            for n in range(step // plan.channels):
                s = c // plan.channels + n
                part = value[:, n * plan.channels : (n + 1) * plan.channels]
                out_ref[:, 0, pl.ds(2 * SUB * s + parity, SUB, stride=2), :] = part.reshape(
                    count, SUB, plan.channels
                )


def own_kernel(plan, place_ref, *refs):
    n = plan.lag_total
    pieces, tabs, (left_ref, right_ref) = refs[:n], refs[n : n + 3], refs[n + 3 : n + 5]
    held, even, odd, ahead, *rest = refs[n + 5 :]
    make_series(plan, place_ref, pieces, tabs, held, even, odd, ahead, right_ref)
    make_left(plan, even, odd, rest[:2], rest[2:], left_ref)


def first_kernel(plan, count, left_ref, right_ref, out_ref):
    correlate(plan, count, left_ref, right_ref, out_ref)


def other_kernel(plan, count, place_ref, *refs):
    n = plan.lag_total
    pieces, tabs, left_ref, out_ref = refs[:n], refs[n : n + 3], refs[n + 3], refs[n + 5]
    held, even, odd, ahead, right = refs[n + 6 :]

    @pl.when(pl.program_id(0) == 0)
    def _():
        make_series(plan, place_ref, pieces, tabs, held, even, odd, ahead, right)

    correlate(plan, count, left_ref, right, out_ref)


def series_scratch(plan):
    return [pltpu.VMEM((plan.joined, plan.wide), BF16)] + [pltpu.VMEM((plan.padded, plan.wide), F32)] * 3


def prepare_own(plan, place, pieces, tabs):
    return pl.pallas_call(
        functools.partial(own_kernel, plan),
        out_shape=(
            jax.ShapeDtypeStruct((3, plan.channels * SUB, plan.deep), BF16),
            jax.ShapeDtypeStruct((3, plan.deep, plan.shifts * plan.channels), BF16),
        ),
        in_specs=[SMEM] + [VMEM] * (plan.lag_total + 3),
        out_specs=(VMEM, VMEM),
        scratch_shapes=series_scratch(plan)
        + [pltpu.VMEM((SUB + plan.deep, plan.channels), F32)] * 2
        + [pltpu.VMEM((2, plan.channels * SUB, LANES), F32)] * 2,
        compiler_params=pltpu.CompilerParams(vmem_limit_bytes=33 * 2**20),
        cost_estimate=pl.CostEstimate(flops=100_000_000, bytes_accessed=2**18, transcendentals=0),
        name="prepare_own",
    )(place, *pieces, *tabs)


def correlation_parts(plan, count, pairs, distance):
    out_shape = jax.ShapeDtypeStruct((plan.channels, pairs, plan.lags, plan.channels), F32)
    out_spec = pl.BlockSpec((count, 1, plan.lags, plan.channels), lambda i: (i, distance, 0, 0))
    flops = 2 * 3 * plan.channels * SUB * plan.deep * plan.shifts * plan.channels
    cost = pl.CostEstimate(flops=flops, bytes_accessed=8 * 2**20, transcendentals=0)
    return out_shape, out_spec, cost


def own_correlation(plan, count, pairs, left, right):
    out_shape, out_spec, cost = correlation_parts(plan, count, pairs, 0)
    return pl.pallas_call(
        functools.partial(first_kernel, plan, count),
        grid=(plan.channels // count,),
        out_shape=out_shape,
        in_specs=[VMEM, VMEM],
        out_specs=out_spec,
        compiler_params=pltpu.CompilerParams(vmem_limit_bytes=24 * 2**20),
        cost_estimate=cost,
        name="own_correlation",
    )(left, right)


def other_correlation(plan, count, pairs, distance, place, pieces, tabs, left, out):
    out_shape, out_spec, cost = correlation_parts(plan, count, pairs, distance)
    in_specs = [SMEM] + [VMEM] * (plan.lag_total + 4) + [pl.BlockSpec(memory_space=pl.ANY)]
    return pl.pallas_call(
        functools.partial(other_kernel, plan, count),
        grid=(plan.channels // count,),
        out_shape=out_shape,
        in_specs=in_specs,
        out_specs=out_spec,
        scratch_shapes=series_scratch(plan)
        + [pltpu.VMEM((3, plan.deep, plan.shifts * plan.channels), BF16)],
        input_output_aliases={len(in_specs) - 1: 0},
        compiler_params=pltpu.CompilerParams(vmem_limit_bytes=30 * 2**20),
        cost_estimate=cost,
        name="other_correlation",
    )(place, *pieces, *tabs, left, out)


def swap(piece, mask):
    count = lax.axis_size("lag")
    return lax.ppermute(piece, "lag", [(i ^ mask, i) for i in range(count)])


def from_ahead(piece, distance):
    count = lax.axis_size("chan")
    return lax.ppermute(piece, "chan", [((i + distance) % count, i) for i in range(count)])


def same_core(piece, start=None, stop=None):
    masks = list(range(0, lax.axis_size("lag"), 2))[start:stop]
    return [swap(piece, mask) if mask else piece for mask in masks]


def both_cores(held):
    return [x for piece in held for x in (piece, swap(piece, 1))]


def shards(raw_samples, decimation_taps, bandpass_taps):
    plan = Plan(raw_samples.shape, lax.axis_size("lag"), decimation_taps.shape[0], bandpass_taps.shape[0])
    pairs = lax.axis_size("chan") // 2 + 1
    place = lax.axis_index("lag").astype(jnp.int32).reshape(1)
    dec_taps = decimation_taps.reshape(1, -1)
    piece, kept = local_rows(plan, raw_samples, dec_taps)
    tabs = tables(plan, dec_taps, bandpass_taps.reshape(1, -1))
    count = 32
    own = same_core(piece)
    far = [from_ahead(piece, distance) for distance in range(1, pairs)]
    tabs, own[1:] = lax.optimization_barrier((tabs, own[1:]))
    pieces, far[0] = lax.optimization_barrier((both_cores(own), far[0]))
    left, right = prepare_own(plan, place, [kept, *pieces[1:]], tabs)
    left, far = lax.optimization_barrier((left, far))
    held = same_core(far[0])
    early = same_core(far[1], stop=-1) if pairs > 2 else None
    out = own_correlation(plan, count, pairs, left, right)
    for distance in range(1, pairs):
        out, held, far = lax.optimization_barrier((out, held, far))
        pieces = both_cores(held)
        if distance + 1 < pairs:
            held = early + same_core(far[distance], start=-1) if distance == 1 else same_core(far[distance])
        out = other_correlation(plan, count, pairs, distance, place, pieces, tabs, left, out)
    return out


def solution(mesh):
    placed = (P(None, "chan", "lag"), P(), P())
    return jax.shard_map(
        shards, mesh=mesh, in_specs=placed, out_specs=P("chan", None, "lag", None), check_vma=False
    )
```

```python
import functools
import math

import jax
import jax.numpy as jnp
from jax import lax
from jax.experimental import pallas as pl
from jax.experimental.pallas import tpu as pltpu
from jax.sharding import PartitionSpec as P

NLAG = 512
SUB = 8
PITCH = SUB + 1
LANES = 128
F32 = jnp.float32
BF16 = jnp.bfloat16
SMEM = pl.BlockSpec(memory_space=pltpu.SMEM)
VMEM = pl.BlockSpec(memory_space=pltpu.VMEM)


def ceil_to(value, unit):
    return -(-value // unit) * unit


class Plan:
    def __init__(self, shape, lag_total, dec_taps, bp_taps):
        self.windows, self.channels, self.raw = shape
        self.lag_total = lag_total
        self.dec_taps, self.bp_taps = dec_taps, bp_taps
        self.dec = self.raw // 2
        self.head = dec_taps // 2
        self.whole = self.dec - self.head
        self.edge = dec_taps - 1
        self.rows = ceil_to(self.whole + 2 * self.edge, SUB)
        self.slot = ceil_to(self.rows, 16)
        self.wide = self.windows * self.channels
        self.total = self.dec * lag_total
        self.half = self.total // 2
        self.depth = ceil_to(self.half + SUB, 16)
        self.deep = self.windows * self.depth
        self.even = self.deep // (2 * LANES) * 2 * LANES
        self.full = 2 * self.deep - self.even
        self.lags = NLAG // lag_total
        self.shifts = self.lags // 2 // SUB
        self.held = lag_total * self.slot
        self.joined = self.held + ceil_to(lag_total * self.head, 16)
        self.pad = NLAG // 4
        self.padded = ceil_to(self.pad + self.depth + NLAG // 4, SUB)


def rounded_tap(taps, index):
    return taps[0:1, index : index + 1].astype(BF16).astype(F32)


def local_kernel(plan, taps_ref, raw_ref, out_ref, spread):
    row = lax.broadcasted_iota(jnp.int32, (plan.rows, plan.raw), 0)
    time = lax.broadcasted_iota(jnp.int32, (plan.rows, plan.raw), 1)
    tap = 2 * (row + plan.head) - time
    table = jnp.zeros((plan.rows, plan.raw), F32)
    for k in range(plan.dec_taps):
        table = jnp.where(tap == k, rounded_tap(taps_ref, k), table)
    last = time - (plan.raw - plan.edge) == row - plan.whole
    first = time == row - plan.whole - plan.edge
    is_last = (row >= plan.whole) & (row < plan.whole + plan.edge)
    is_first = (row >= plan.whole + plan.edge) & (row < plan.whole + 2 * plan.edge)
    picked = jnp.where(is_last & last | is_first & first, 1.0, 0.0)
    table = jnp.where(row < plan.whole, table, picked).astype(BF16)
    spread[...] = raw_ref[...].astype(F32).reshape(plan.raw * plan.windows, plan.channels)
    series = [
        spread[pl.ds(w, plan.raw, stride=plan.windows), :].astype(BF16) for w in range(plan.windows)
    ]
    out_ref[...] = jnp.dot(
        table, jnp.concatenate(series, axis=1), preferred_element_type=F32
    ).astype(BF16)


def local_rows(plan, raw, taps):
    return pl.pallas_call(
        functools.partial(local_kernel, plan),
        out_shape=jax.ShapeDtypeStruct((plan.rows, plan.wide), BF16),
        in_specs=[VMEM, VMEM],
        out_specs=VMEM,
        scratch_shapes=[pltpu.VMEM((plan.raw * plan.windows, plan.channels), F32)],
        name="local_rows",
    )(taps, jnp.transpose(raw, (2, 0, 1)))


def table_kernel(plan, dec_ref, bp_ref, piece_ref, band_ref, edge_ref, kept_ref):
    kept_ref[...] = piece_ref[...]
    span = ceil_to(plan.total + plan.bp_taps, LANES)
    lane = lax.broadcasted_iota(jnp.int32, (1, span), 1)
    base = jnp.zeros((1, span), F32)
    for k in range(plan.bp_taps):
        base = jnp.where(lane == (span - k) % span, rounded_tap(bp_ref, k), base)
    col = lax.broadcasted_iota(jnp.int32, (span, plan.joined), 1)
    time = lax.broadcasted_iota(jnp.int32, (span, plan.joined), 0)
    at = jnp.full((span, plan.joined), -1, jnp.int32)
    for p in range(plan.lag_total):
        start = col - p * plan.slot
        at = jnp.where((start >= 0) & (start < plan.whole), start + p * plan.dec + plan.head, at)
        start = col - plan.held - p * plan.head
        at = jnp.where((start >= 0) & (start < plan.head), start + p * plan.dec, at)
    order = jnp.where(time == at, 1.0, 0.0).astype(BF16)
    for parity in range(2):
        spread = jnp.broadcast_to(base, (plan.half, span))
        taps = pltpu.roll(spread, parity, 1, stride=2, stride_axis=0)
        band_ref[parity * plan.half : (parity + 1) * plan.half, :] = jnp.dot(taps.astype(BF16), order, preferred_element_type=F32).astype(BF16)
    rows = plan.joined - plan.held
    row = lax.broadcasted_iota(jnp.int32, (rows, plan.held), 0)
    col = lax.broadcasted_iota(jnp.int32, (rows, plan.held), 1)
    tap = jnp.full((rows, plan.held), -1, jnp.int32)
    for p in range(plan.lag_total):
        j = row - p * plan.head
        mine = (j >= 0) & (j < plan.head)
        r = col - p * plan.slot - plan.whole - plan.edge
        tap = jnp.where(mine & (r >= 0) & (r < plan.edge), 2 * j - r, tap)
        r = col - (p - 1) * plan.slot - plan.whole
        tap = jnp.where(mine & (r >= 0) & (r < plan.edge), 2 * j + plan.edge - r, tap)
    table = jnp.zeros((rows, plan.held), F32)
    for k in range(plan.dec_taps):
        table = jnp.where(tap == k, rounded_tap(dec_ref, k), table)
    edge_ref[...] = table.astype(BF16)


def tables(plan, dec_taps, bp_taps, piece):
    return pl.pallas_call(
        functools.partial(table_kernel, plan),
        out_shape=(
            jax.ShapeDtypeStruct((2 * plan.half, plan.joined), BF16),
            jax.ShapeDtypeStruct((plan.joined - plan.held, plan.held), BF16),
            jax.ShapeDtypeStruct(piece.shape, piece.dtype),
        ),
        in_specs=[VMEM, VMEM, VMEM],
        out_specs=(VMEM, VMEM, VMEM),
        compiler_params=pltpu.CompilerParams(vmem_limit_bytes=12 * 2**20),
        cost_estimate=pl.CostEstimate(flops=500_000_000, bytes_accessed=2_000_000, transcendentals=0),
        name="tables",
    )(dec_taps, bp_taps, piece)


def make_series(plan, place_ref, pieces, tables_refs, held, even, odd, ahead, right):
    place = place_ref[0]
    if plan.slot > plan.rows:
        for p in range(plan.lag_total):
            held[(p + 1) * plan.slot - 16 : (p + 1) * plan.slot, :] = jnp.zeros((16, plan.wide), BF16)
    places = [
        pl.ds(pl.multiple_of(lax.bitwise_xor(place, p) * plan.slot, 16), plan.rows)
        for p in range(plan.lag_total)
    ]
    for p, piece in enumerate(pieces):
        held[places[p], :] = piece[...]
    for ref in (even, odd, ahead):
        ref[0 : plan.pad, :] = jnp.zeros((plan.pad, plan.wide), F32)
        ref[plan.pad + plan.half - SUB :, :] = jnp.zeros(
            (plan.padded - plan.pad - plan.half + SUB, plan.wide), F32
        )
    filter_block(plan, tables_refs, held, even, odd, ahead)
    lay_right(plan, place, even, odd, ahead, right)


def filter_block(plan, tables_refs, held, even, odd, ahead):
    band_ref, edge_ref = tables_refs
    held[plan.held : plan.joined, :] = jnp.dot(
        edge_ref[...], held[0 : plan.held, :], preferred_element_type=F32
    ).astype(BF16)
    step = 2 * LANES
    for c in range(0, plan.wide, step):
        cols = slice(c, c + step)
        block = held[:, cols]
        both = jnp.dot(band_ref[...], block, preferred_element_type=F32)
        a, b = both[0 : plan.half], both[plan.half :]
        power = jnp.sum(a * a + b * b, axis=0, keepdims=True) * (1.0 / plan.total)
        scale = lax.rsqrt(power + 1e-06)
        a = (a * scale).astype(BF16).astype(F32)
        b = (b * scale).astype(BF16).astype(F32)
        even[plan.pad : plan.pad + plan.half, cols] = a
        odd[plan.pad : plan.pad + plan.half, cols] = b
        ahead[plan.pad - 1 : plan.pad - 1 + plan.half, cols] = a


def lay_right(plan, place, even, odd, ahead, right):
    base = place * (plan.lags // 2)
    for w in range(plan.windows):
        cols = slice(w * plan.channels, (w + 1) * plan.channels)
        rows = slice(w * plan.depth, (w + 1) * plan.depth)
        for first in range(2):
            shifts = range(first, plan.shifts, 2)
            height = plan.depth + 2 * SUB * (len(shifts) - 1)
            at = pl.ds(pl.multiple_of(base + first * SUB, SUB), height)
            a, b, c = even[at, cols], odd[at, cols], ahead[at, cols]
            for k, value in enumerate((b, a - b, c - b)):
                value = value.astype(BF16)
                for n, s in enumerate(shifts):
                    to = slice(s * plan.channels, (s + 1) * plan.channels)
                    part = value[2 * SUB * n : 2 * SUB * n + plan.depth]
                    over = max(0, rows.stop - max(rows.start, plan.even)) if k == 0 else 0
                    if over < plan.depth:
                        right[k, rows.start : rows.stop - over, to] = part[: plan.depth - over]
                    if over:
                        first_over = rows.stop - over - plan.even + plan.deep
                        for other in (1, 2):
                            right[other, first_over : first_over + over, to] = part[plan.depth - over :]


def make_left(plan, even, odd, stacks, mixes, left):
    for ref, stack in zip((even, odd), stacks, strict=True):
        stack[0:SUB, :] = jnp.zeros((SUB, plan.channels), F32)
        for w in range(plan.windows):
            stack[SUB + w * plan.depth : SUB + (w + 1) * plan.depth, :] = ref[
                plan.pad : plan.pad + plan.depth, w * plan.channels : (w + 1) * plan.channels
            ]
    for n, c in enumerate(range(0, plan.deep, LANES)):
        mixed = mixes[n % len(mixes)]
        for delay in range(SUB):
            rows = slice(SUB - delay + c, SUB - delay + c + LANES)
            for e, stack in enumerate(stacks):
                mixed[e, pl.ds(delay, plan.channels, stride=PITCH), :] = stack[rows, :].T
        for r in range(0, plan.channels * SUB, LANES):
            a, b = (
                jnp.concatenate(
                    [mixed[e, i * PITCH : i * PITCH + SUB, :] for i in range(r // SUB, (r + LANES) // SUB)], axis=0
                )
                for e in range(2)
            )
            for k, value in enumerate((a + b, a, b)):
                value = value.astype(BF16)
                if k > 0 or c < plan.even:
                    left[k, r : r + LANES, c : c + LANES] = value
                else:
                    for other in (1, 2):
                        at = c - plan.even + plan.deep
                        left[other, r : r + LANES, at : at + LANES] = value


def correlate(plan, count, left, right, out_ref):
    factor = 1.0 / math.sqrt(plan.windows * plan.total)
    step = min(2 * LANES, plan.shifts * plan.channels)
    for c in range(0, plan.shifts * plan.channels, step):
        cols = slice(c, c + step)
        rows = pl.ds(pl.multiple_of(pl.program_id(0) * count * SUB, count * SUB), count * SUB)
        both, even, odd = (
            jnp.dot(left[k, rows, :deep], right[k, :deep, cols], preferred_element_type=F32)
            for k, deep in enumerate((plan.even, plan.full, plan.full))
        )
        for parity, value in ((0, even), (1, odd)):
            value = (both + value) * factor
            for n in range(step // plan.channels):
                s = c // plan.channels + n
                part = value[:, n * plan.channels : (n + 1) * plan.channels]
                out_ref[:, 0, pl.ds(2 * SUB * s + parity, SUB, stride=2), :] = part.reshape(
                    count, SUB, plan.channels
                )


def own_kernel(plan, place_ref, *refs):
    n = plan.lag_total
    pieces, tabs, (left_ref, right_ref) = refs[:n], refs[n : n + 2], refs[n + 2 : n + 4]
    held, even, odd, ahead, *rest = refs[n + 4 :]
    make_series(plan, place_ref, pieces, tabs, held, even, odd, ahead, right_ref)
    make_left(plan, even, odd, rest[:2], rest[2:], left_ref)


def first_kernel(plan, count, left_ref, right_ref, out_ref):
    correlate(plan, count, left_ref, right_ref, out_ref)


def other_kernel(plan, count, place_ref, *refs):
    n = plan.lag_total
    pieces, tabs, left_ref, out_ref = refs[:n], refs[n : n + 2], refs[n + 2], refs[n + 4]
    held, even, odd, ahead, right = refs[n + 5 :]

    @pl.when(pl.program_id(0) == 0)
    def _():
        make_series(plan, place_ref, pieces, tabs, held, even, odd, ahead, right)

    correlate(plan, count, left_ref, right, out_ref)


def series_scratch(plan):
    return [pltpu.VMEM((plan.joined, plan.wide), BF16)] + [pltpu.VMEM((plan.padded, plan.wide), F32)] * 3


def prepare_own(plan, place, pieces, tabs):
    return pl.pallas_call(
        functools.partial(own_kernel, plan),
        out_shape=(
            jax.ShapeDtypeStruct((3, plan.channels * SUB, plan.full), BF16),
            jax.ShapeDtypeStruct((3, plan.full, plan.shifts * plan.channels), BF16),
        ),
        in_specs=[SMEM] + [VMEM] * (plan.lag_total + 2),
        out_specs=(VMEM, VMEM),
        scratch_shapes=series_scratch(plan)
        + [pltpu.VMEM((SUB + plan.deep, plan.channels), F32)] * 2
        + [pltpu.VMEM((2, plan.channels * PITCH, LANES), F32)],
        compiler_params=pltpu.CompilerParams(vmem_limit_bytes=33 * 2**20),
        cost_estimate=pl.CostEstimate(flops=100_000_000, bytes_accessed=2**18, transcendentals=0),
        name="prepare_own",
    )(place, *pieces, *tabs)


def correlation_parts(plan, count, pairs, distance):
    out_shape = jax.ShapeDtypeStruct((plan.channels, pairs, plan.lags, plan.channels), F32)
    out_spec = pl.BlockSpec((count, 1, plan.lags, plan.channels), lambda i: (i, distance, 0, 0))
    flops = 2 * 3 * plan.channels * SUB * plan.deep * plan.shifts * plan.channels
    cost = pl.CostEstimate(flops=flops, bytes_accessed=8 * 2**20, transcendentals=0)
    return out_shape, out_spec, cost


def own_correlation(plan, count, pairs, left, right):
    out_shape, out_spec, cost = correlation_parts(plan, count, pairs, 0)
    return pl.pallas_call(
        functools.partial(first_kernel, plan, count),
        grid=(plan.channels // count,),
        out_shape=out_shape,
        in_specs=[VMEM, VMEM],
        out_specs=out_spec,
        compiler_params=pltpu.CompilerParams(vmem_limit_bytes=24 * 2**20),
        cost_estimate=cost,
        name="own_correlation",
    )(left, right)


def other_correlation(plan, count, pairs, distance, place, pieces, tabs, left, out):
    out_shape, out_spec, cost = correlation_parts(plan, count, pairs, distance)
    in_specs = [SMEM] + [VMEM] * (plan.lag_total + 3) + [pl.BlockSpec(memory_space=pl.ANY)]
    return pl.pallas_call(
        functools.partial(other_kernel, plan, count),
        grid=(plan.channels // count,),
        out_shape=out_shape,
        in_specs=in_specs,
        out_specs=out_spec,
        scratch_shapes=series_scratch(plan)
        + [pltpu.VMEM((3, plan.full, plan.shifts * plan.channels), BF16)],
        input_output_aliases={len(in_specs) - 1: 0},
        compiler_params=pltpu.CompilerParams(vmem_limit_bytes=30 * 2**20),
        cost_estimate=cost,
        name="other_correlation",
    )(place, *pieces, *tabs, left, out)


def swap(piece, mask):
    count = lax.axis_size("lag")
    return lax.ppermute(piece, "lag", [(i ^ mask, i) for i in range(count)])


def from_ahead(piece, distance):
    count = lax.axis_size("chan")
    return lax.ppermute(piece, "chan", [((i + distance) % count, i) for i in range(count)])


def same_core(piece):
    return [swap(piece, mask) if mask else piece for mask in range(0, lax.axis_size("lag"), 2)]


def both_cores(held):
    return [x for piece in held for x in (piece, swap(piece, 1))]


def shards(raw_samples, decimation_taps, bandpass_taps):
    plan = Plan(raw_samples.shape, lax.axis_size("lag"), decimation_taps.shape[0], bandpass_taps.shape[0])
    pairs = lax.axis_size("chan") // 2 + 1
    place = lax.axis_index("lag").astype(jnp.int32).reshape(1)
    dec_taps = decimation_taps.reshape(1, -1)
    piece = local_rows(plan, raw_samples, dec_taps)
    *tabs, kept = tables(plan, dec_taps, bandpass_taps.reshape(1, -1), piece)
    count = 32
    own = same_core(piece)
    near = from_ahead(piece, 1)
    tabs, own[1:] = lax.optimization_barrier((tabs, own[1:]))
    pieces, near = lax.optimization_barrier((both_cores(own), near))
    left, right = prepare_own(plan, place, [kept, *pieces[1:]], tabs)
    left, near, piece = lax.optimization_barrier((left, near, piece))
    held = same_core(near)
    far = {distance: from_ahead(piece, distance) for distance in range(2, pairs)}
    out = own_correlation(plan, count, pairs, left, right)
    for distance in range(1, pairs):
        out, held, far = lax.optimization_barrier((out, held, far))
        pieces = both_cores(held)
        if distance + 1 < pairs:
            held = same_core(far[distance + 1])
        out = other_correlation(plan, count, pairs, distance, place, pieces, tabs, left, out)
    return out


def solution(mesh):
    placed = (P(None, "chan", "lag"), P(), P())
    return jax.shard_map(
        shards, mesh=mesh, in_specs=placed, out_specs=P("chan", None, "lag", None), check_vma=False
    )
```

```python
import functools
import math

import jax
import jax.numpy as jnp
from jax import lax
from jax.experimental import pallas as pl
from jax.experimental.pallas import tpu as pltpu
from jax.sharding import PartitionSpec as P

NLAG = 512
SUB = 8
PITCH = SUB + 1
LANES = 128
F32 = jnp.float32
BF16 = jnp.bfloat16
SMEM = pl.BlockSpec(memory_space=pltpu.SMEM)
VMEM = pl.BlockSpec(memory_space=pltpu.VMEM)


def ceil_to(value, unit):
    return -(-value // unit) * unit


class Plan:
    def __init__(self, shape, lag_total, dec_taps, bp_taps):
        self.windows, self.channels, self.raw = shape
        self.lag_total = lag_total
        self.dec_taps, self.bp_taps = dec_taps, bp_taps
        self.dec = self.raw // 2
        self.head = dec_taps // 2
        self.whole = self.dec - self.head
        self.edge = dec_taps - 1
        self.rows = ceil_to(self.whole + 2 * self.edge, SUB)
        self.slot = ceil_to(self.rows, 16)
        self.wide = self.windows * self.channels
        self.total = self.dec * lag_total
        self.half = self.total // 2
        self.depth = ceil_to(self.half + SUB, 16)
        self.deep = self.windows * self.depth
        self.even = self.deep // (2 * LANES) * 2 * LANES
        self.full = 2 * self.deep - self.even
        self.lags = NLAG // lag_total
        self.shifts = self.lags // 2 // SUB
        self.pitch = self.depth + 2 * SUB * (self.shifts // 2 - 1)
        self.held = lag_total * self.slot
        self.joined = self.held + ceil_to(lag_total * self.head, 16)
        self.pad = NLAG // 4
        self.padded = ceil_to(self.pad + self.depth + NLAG // 4, SUB)


def rounded_tap(taps, index):
    return taps[0:1, index : index + 1].astype(BF16).astype(F32)


def local_kernel(plan, taps_ref, bp_ref, raw_ref, out_ref, kept_ref, spread, both):
    row = lax.broadcasted_iota(jnp.int32, (plan.rows, plan.raw), 0)
    time = lax.broadcasted_iota(jnp.int32, (plan.rows, plan.raw), 1)
    tap = 2 * (row + plan.head) - time
    table = jnp.zeros((plan.rows, plan.raw), F32)
    for k in range(plan.dec_taps):
        table = jnp.where(tap == k, rounded_tap(taps_ref, k), table)
    last = time - (plan.raw - plan.edge) == row - plan.whole
    first = time == row - plan.whole - plan.edge
    is_last = (row >= plan.whole) & (row < plan.whole + plan.edge)
    is_first = (row >= plan.whole + plan.edge) & (row < plan.whole + 2 * plan.edge)
    picked = jnp.where(is_last & last | is_first & first, 1.0, 0.0)
    table = jnp.where(row < plan.whole, table, picked).astype(BF16)
    spread[...] = raw_ref[...].astype(F32).reshape(plan.raw * plan.windows, plan.channels)
    series = [
        spread[pl.ds(w, plan.raw, stride=plan.windows), :].astype(BF16) for w in range(plan.windows)
    ]
    rows = jnp.dot(table, jnp.concatenate(series, axis=1), preferred_element_type=F32).astype(BF16)
    out_ref[...] = rows
    kept_ref[0 : plan.rows, :] = rows
    both[...] = jnp.zeros((SUB, LANES), F32)
    both[0:1, 0 : plan.dec_taps] = taps_ref[...]
    both[1:2, 0 : plan.bp_taps] = bp_ref[...]
    kept_ref[plan.rows :, 0:LANES] = both[...].astype(BF16)


def local_rows(plan, raw, dec_taps, bp_taps):
    return pl.pallas_call(
        functools.partial(local_kernel, plan),
        out_shape=(
            jax.ShapeDtypeStruct((plan.rows, plan.wide), BF16),
            jax.ShapeDtypeStruct((plan.rows + SUB, plan.wide), BF16),
        ),
        in_specs=[VMEM, VMEM, VMEM],
        out_specs=(VMEM, VMEM),
        scratch_shapes=[
            pltpu.VMEM((plan.raw * plan.windows, plan.channels), F32),
            pltpu.VMEM((SUB, LANES), F32),
        ],
        name="local_rows",
    )(dec_taps, bp_taps, jnp.transpose(raw, (2, 0, 1)))


def table_kernel(plan, rows_ref, band_ref, edge_ref, kept_ref):
    kept_ref[...] = rows_ref[0 : plan.rows, :]
    dec_ref, bp_ref = (rows_ref[plan.rows :, 0:LANES].astype(F32)[k : k + 1] for k in range(2))
    span = ceil_to(plan.total + plan.bp_taps, LANES)
    lane = lax.broadcasted_iota(jnp.int32, (1, span), 1)
    base = jnp.zeros((1, span), F32)
    for k in range(plan.bp_taps):
        base = jnp.where(lane == (span - k) % span, rounded_tap(bp_ref, k), base)
    col = lax.broadcasted_iota(jnp.int32, (span, plan.joined), 1)
    time = lax.broadcasted_iota(jnp.int32, (span, plan.joined), 0)
    at = jnp.full((span, plan.joined), -1, jnp.int32)
    for p in range(plan.lag_total):
        start = col - p * plan.slot
        at = jnp.where((start >= 0) & (start < plan.whole), start + p * plan.dec + plan.head, at)
        start = col - plan.held - p * plan.head
        at = jnp.where((start >= 0) & (start < plan.head), start + p * plan.dec, at)
    order = jnp.where(time == at, 1.0, 0.0).astype(BF16)
    for parity in range(2):
        spread = jnp.broadcast_to(base, (plan.half, span))
        taps = pltpu.roll(spread, parity, 1, stride=2, stride_axis=0)
        band_ref[parity * plan.half : (parity + 1) * plan.half, :] = jnp.dot(taps.astype(BF16), order, preferred_element_type=F32).astype(BF16)
    rows = plan.joined - plan.held
    row = lax.broadcasted_iota(jnp.int32, (rows, plan.held), 0)
    col = lax.broadcasted_iota(jnp.int32, (rows, plan.held), 1)
    tap = jnp.full((rows, plan.held), -1, jnp.int32)
    for p in range(plan.lag_total):
        j = row - p * plan.head
        mine = (j >= 0) & (j < plan.head)
        r = col - p * plan.slot - plan.whole - plan.edge
        tap = jnp.where(mine & (r >= 0) & (r < plan.edge), 2 * j - r, tap)
        r = col - (p - 1) * plan.slot - plan.whole
        tap = jnp.where(mine & (r >= 0) & (r < plan.edge), 2 * j + plan.edge - r, tap)
    table = jnp.zeros((rows, plan.held), F32)
    for k in range(plan.dec_taps):
        table = jnp.where(tap == k, rounded_tap(dec_ref, k), table)
    edge_ref[...] = table.astype(BF16)


def tables(plan, rows):
    return pl.pallas_call(
        functools.partial(table_kernel, plan),
        out_shape=(
            jax.ShapeDtypeStruct((2 * plan.half, plan.joined), BF16),
            jax.ShapeDtypeStruct((plan.joined - plan.held, plan.held), BF16),
            jax.ShapeDtypeStruct((plan.rows, plan.wide), BF16),
        ),
        in_specs=[VMEM],
        out_specs=(VMEM, VMEM, VMEM),
        compiler_params=pltpu.CompilerParams(vmem_limit_bytes=12 * 2**20),
        cost_estimate=pl.CostEstimate(flops=500_000_000, bytes_accessed=2_000_000, transcendentals=0),
        name="tables",
    )(rows)


def make_series(plan, place_ref, pieces, tables_refs, held, even, odd, ahead, right):
    place = place_ref[0]
    if plan.slot > plan.rows:
        for p in range(plan.lag_total):
            held[(p + 1) * plan.slot - 16 : (p + 1) * plan.slot, :] = jnp.zeros((16, plan.wide), BF16)
    places = [
        pl.ds(pl.multiple_of(lax.bitwise_xor(place, p) * plan.slot, 16), plan.rows)
        for p in range(plan.lag_total)
    ]
    for p, piece in enumerate(pieces):
        held[places[p], :] = piece[...]
    for ref in (even, odd, ahead):
        ref[0 : plan.pad, :] = jnp.zeros((plan.pad, plan.wide), F32)
        ref[plan.pad + plan.half - SUB :, :] = jnp.zeros(
            (plan.padded - plan.pad - plan.half + SUB, plan.wide), F32
        )
    filter_block(plan, tables_refs, held, even, odd, ahead)
    lay_right(plan, place, even, odd, ahead, right)


def filter_block(plan, tables_refs, held, even, odd, ahead):
    band_ref, edge_ref = tables_refs
    held[plan.held : plan.joined, :] = jnp.dot(
        edge_ref[...], held[0 : plan.held, :], preferred_element_type=F32
    ).astype(BF16)
    step = 2 * LANES
    for c in range(0, plan.wide, step):
        cols = slice(c, c + step)
        block = held[:, cols]
        both = jnp.dot(band_ref[...], block, preferred_element_type=F32)
        a, b = both[0 : plan.half], both[plan.half :]
        power = jnp.sum(a * a + b * b, axis=0, keepdims=True) * (1.0 / plan.total)
        scale = lax.rsqrt(power + 1e-06)
        a = (a * scale).astype(BF16).astype(F32)
        b = (b * scale).astype(BF16).astype(F32)
        even[plan.pad : plan.pad + plan.half, cols] = a
        odd[plan.pad : plan.pad + plan.half, cols] = b
        ahead[plan.pad - 1 : plan.pad - 1 + plan.half, cols] = a


def lay_right(plan, place, even, odd, ahead, right):
    base = place * (plan.lags // 2)
    for w in range(plan.windows):
        cols = slice(w * plan.channels, (w + 1) * plan.channels)
        for first in range(2):
            at = pl.ds(pl.multiple_of(base + first * SUB, SUB), plan.pitch)
            a, b, c = even[at, cols], odd[at, cols], ahead[at, cols]
            to = slice(first * plan.channels, (first + 1) * plan.channels)
            for k, value in enumerate((b, a - b, c - b)):
                right[k, w * plan.pitch : (w + 1) * plan.pitch, to] = value.astype(BF16)


def right_operand(plan, k, n, right):
    def rows(k, low, high):
        parts = []
        for w in range(plan.windows):
            start, stop = max(low, w * plan.depth), min(high, (w + 1) * plan.depth)
            if start < stop:
                at = w * (plan.pitch - plan.depth) + 2 * SUB * n
                parts.append(right[k, at + start : at + stop, :])
        return parts

    if k == 0:
        return jnp.concatenate(rows(0, 0, plan.even), axis=0)
    return jnp.concatenate(rows(k, 0, plan.deep) + rows(0, plan.even, plan.deep), axis=0)


def make_left(plan, even, odd, stacks, mixes, left):
    for ref, stack in zip((even, odd), stacks, strict=True):
        stack[0:SUB, :] = jnp.zeros((SUB, plan.channels), F32)
        for w in range(plan.windows):
            stack[SUB + w * plan.depth : SUB + (w + 1) * plan.depth, :] = ref[
                plan.pad : plan.pad + plan.depth, w * plan.channels : (w + 1) * plan.channels
            ]
    for n, c in enumerate(range(0, plan.deep, LANES)):
        mixed = mixes[n % len(mixes)]
        for delay in range(SUB):
            rows = slice(SUB - delay + c, SUB - delay + c + LANES)
            for e, stack in enumerate(stacks):
                mixed[e, pl.ds(delay, plan.channels, stride=PITCH), :] = stack[rows, :].T
        for r in range(0, plan.channels * SUB, LANES):
            a, b = (
                jnp.concatenate(
                    [mixed[e, i * PITCH : i * PITCH + SUB, :] for i in range(r // SUB, (r + LANES) // SUB)], axis=0
                )
                for e in range(2)
            )
            for k, value in enumerate((a + b, a, b)):
                value = value.astype(BF16)
                if k > 0 or c < plan.even:
                    left[k, r : r + LANES, c : c + LANES] = value
                else:
                    for other in (1, 2):
                        at = c - plan.even + plan.deep
                        left[other, r : r + LANES, at : at + LANES] = value


def correlate(plan, count, left, right, out_ref):
    factor = 1.0 / math.sqrt(plan.windows * plan.total)
    for n in range(plan.shifts // 2):
        rows = pl.ds(pl.multiple_of(pl.program_id(0) * count * SUB, count * SUB), count * SUB)
        both, even, odd = (
            jnp.dot(left[k, rows, :deep], right_operand(plan, k, n, right), preferred_element_type=F32)
            for k, deep in enumerate((plan.even, plan.full, plan.full))
        )
        for parity, value in ((0, even), (1, odd)):
            value = (both + value) * factor
            for first in range(2):
                s = 2 * n + first
                part = value[:, first * plan.channels : (first + 1) * plan.channels]
                out_ref[:, 0, pl.ds(2 * SUB * s + parity, SUB, stride=2), :] = part.reshape(
                    count, SUB, plan.channels
                )


def own_kernel(plan, place_ref, *refs):
    n = plan.lag_total
    pieces, tabs, (left_ref, right_ref) = refs[:n], refs[n : n + 2], refs[n + 2 : n + 4]
    held, even, odd, ahead, *rest = refs[n + 4 :]
    make_series(plan, place_ref, pieces, tabs, held, even, odd, ahead, right_ref)
    make_left(plan, even, odd, rest[:2], rest[2:], left_ref)


def first_kernel(plan, count, left_ref, right_ref, out_ref):
    correlate(plan, count, left_ref, right_ref, out_ref)


def other_kernel(plan, count, place_ref, *refs):
    n = plan.lag_total
    pieces, tabs, left_ref, out_ref = refs[:n], refs[n : n + 2], refs[n + 2], refs[n + 4]
    held, even, odd, ahead, right = refs[n + 5 :]

    @pl.when(pl.program_id(0) == 0)
    def _():
        make_series(plan, place_ref, pieces, tabs, held, even, odd, ahead, right)

    correlate(plan, count, left_ref, right, out_ref)


def series_scratch(plan):
    return [pltpu.VMEM((plan.joined, plan.wide), BF16)] + [pltpu.VMEM((plan.padded, plan.wide), F32)] * 3


def prepare_own(plan, place, pieces, tabs):
    return pl.pallas_call(
        functools.partial(own_kernel, plan),
        out_shape=(
            jax.ShapeDtypeStruct((3, plan.channels * SUB, plan.full), BF16),
            jax.ShapeDtypeStruct((3, plan.windows * plan.pitch, 2 * plan.channels), BF16),
        ),
        in_specs=[SMEM] + [VMEM] * (plan.lag_total + 2),
        out_specs=(VMEM, VMEM),
        scratch_shapes=series_scratch(plan)
        + [pltpu.VMEM((SUB + plan.deep, plan.channels), F32)] * 2
        + [pltpu.VMEM((2, plan.channels * PITCH, LANES), F32)],
        compiler_params=pltpu.CompilerParams(vmem_limit_bytes=33 * 2**20),
        cost_estimate=pl.CostEstimate(flops=100_000_000, bytes_accessed=2**18, transcendentals=0),
        name="prepare_own",
    )(place, *pieces, *tabs)


def correlation_parts(plan, count, pairs, distance):
    out_shape = jax.ShapeDtypeStruct((plan.channels, pairs, plan.lags, plan.channels), F32)
    out_spec = pl.BlockSpec((count, 1, plan.lags, plan.channels), lambda i: (i, distance, 0, 0))
    flops = 2 * 3 * plan.channels * SUB * plan.deep * plan.shifts * plan.channels
    cost = pl.CostEstimate(flops=flops, bytes_accessed=8 * 2**20, transcendentals=0)
    return out_shape, out_spec, cost


def own_correlation(plan, count, pairs, left, right):
    out_shape, out_spec, cost = correlation_parts(plan, count, pairs, 0)
    return pl.pallas_call(
        functools.partial(first_kernel, plan, count),
        grid=(plan.channels // count,),
        out_shape=out_shape,
        in_specs=[VMEM, VMEM],
        out_specs=out_spec,
        compiler_params=pltpu.CompilerParams(vmem_limit_bytes=24 * 2**20),
        cost_estimate=cost,
        name="own_correlation",
    )(left, right)


def other_correlation(plan, count, pairs, distance, place, pieces, tabs, left, out):
    out_shape, out_spec, cost = correlation_parts(plan, count, pairs, distance)
    in_specs = [SMEM] + [VMEM] * (plan.lag_total + 3) + [pl.BlockSpec(memory_space=pl.ANY)]
    return pl.pallas_call(
        functools.partial(other_kernel, plan, count),
        grid=(plan.channels // count,),
        out_shape=out_shape,
        in_specs=in_specs,
        out_specs=out_spec,
        scratch_shapes=series_scratch(plan)
        + [pltpu.VMEM((3, plan.windows * plan.pitch, 2 * plan.channels), BF16)],
        input_output_aliases={len(in_specs) - 1: 0},
        compiler_params=pltpu.CompilerParams(vmem_limit_bytes=30 * 2**20),
        cost_estimate=cost,
        name="other_correlation",
    )(place, *pieces, *tabs, left, out)


def swap(piece, mask):
    count = lax.axis_size("lag")
    return lax.ppermute(piece, "lag", [(i ^ mask, i) for i in range(count)])


def from_ahead(piece, distance):
    count = lax.axis_size("chan")
    return lax.ppermute(piece, "chan", [((i + distance) % count, i) for i in range(count)])


def same_core(piece):
    return [swap(piece, mask) if mask else piece for mask in range(0, lax.axis_size("lag"), 2)]


def both_cores(held):
    return [x for piece in held for x in (piece, swap(piece, 1))]


def shards(raw_samples, decimation_taps, bandpass_taps):
    plan = Plan(raw_samples.shape, lax.axis_size("lag"), decimation_taps.shape[0], bandpass_taps.shape[0])
    pairs = lax.axis_size("chan") // 2 + 1
    place = lax.axis_index("lag").astype(jnp.int32).reshape(1)
    piece, kept = local_rows(
        plan, raw_samples, decimation_taps.reshape(1, -1), bandpass_taps.reshape(1, -1)
    )
    *tabs, kept = tables(plan, kept)
    count = 32
    own = same_core(piece)
    near = from_ahead(piece, 1)
    tabs, own[1:] = lax.optimization_barrier((tabs, own[1:]))
    pieces, near = lax.optimization_barrier((both_cores(own), near))
    left, right = prepare_own(plan, place, [kept, *pieces[1:]], tabs)
    left, near, piece = lax.optimization_barrier((left, near, piece))
    held = same_core(near)
    far = {distance: from_ahead(piece, distance) for distance in range(2, pairs)}
    out = own_correlation(plan, count, pairs, left, right)
    for distance in range(1, pairs):
        out, held, far = lax.optimization_barrier((out, held, far))
        pieces = both_cores(held)
        if distance + 1 < pairs:
            held = same_core(far[distance + 1])
        out = other_correlation(plan, count, pairs, distance, place, pieces, tabs, left, out)
    return out


def solution(mesh):
    placed = (P(None, "chan", "lag"), P(), P())
    return jax.shard_map(
        shards, mesh=mesh, in_specs=placed, out_specs=P("chan", None, "lag", None), check_vma=False
    )
```

```python
import functools
import math

import jax
import jax.numpy as jnp
from jax import lax
from jax.experimental import pallas as pl
from jax.experimental.pallas import tpu as pltpu
from jax.sharding import PartitionSpec as P

NLAG = 512
SUB = 8
PITCH = SUB + 1
LANES = 128
F32 = jnp.float32
BF16 = jnp.bfloat16
SMEM = pl.BlockSpec(memory_space=pltpu.SMEM)
VMEM = pl.BlockSpec(memory_space=pltpu.VMEM)


def ceil_to(value, unit):
    return -(-value // unit) * unit


class Plan:
    def __init__(self, shape, lag_total, dec_taps, bp_taps):
        self.windows, self.channels, self.raw = shape
        self.lag_total = lag_total
        self.dec_taps, self.bp_taps = dec_taps, bp_taps
        self.dec = self.raw // 2
        self.head = dec_taps // 2
        self.whole = self.dec - self.head
        self.edge = dec_taps - 1
        self.rows = ceil_to(self.whole + 2 * self.edge, SUB)
        self.slot = ceil_to(self.rows, 16)
        self.wide = self.windows * self.channels
        self.total = self.dec * lag_total
        self.half = self.total // 2
        self.depth = ceil_to(self.half + SUB, 16)
        self.deep = self.windows * self.depth
        self.even = self.deep // (2 * LANES) * 2 * LANES
        self.full = 2 * self.deep - self.even
        self.lags = NLAG // lag_total
        self.shifts = self.lags // 2 // SUB
        self.pitch = self.depth + 2 * SUB * (self.shifts // 2 - 1)
        self.held = lag_total * self.slot
        self.joined = self.held + ceil_to(lag_total * self.head, 16)
        self.pad = NLAG // 4
        self.padded = ceil_to(self.pad + self.depth + NLAG // 4, SUB)


def rounded_tap(taps, index):
    return taps[0:1, index : index + 1].astype(BF16).astype(F32)


def local_kernel(plan, taps_ref, bp_ref, raw_ref, out_ref, kept_ref, spread, both):
    row = lax.broadcasted_iota(jnp.int32, (plan.rows, plan.raw), 0)
    time = lax.broadcasted_iota(jnp.int32, (plan.rows, plan.raw), 1)
    tap = 2 * (row + plan.head) - time
    table = jnp.zeros((plan.rows, plan.raw), F32)
    for k in range(plan.dec_taps):
        table = jnp.where(tap == k, rounded_tap(taps_ref, k), table)
    last = time - (plan.raw - plan.edge) == row - plan.whole
    first = time == row - plan.whole - plan.edge
    is_last = (row >= plan.whole) & (row < plan.whole + plan.edge)
    is_first = (row >= plan.whole + plan.edge) & (row < plan.whole + 2 * plan.edge)
    picked = jnp.where(is_last & last | is_first & first, 1.0, 0.0)
    table = jnp.where(row < plan.whole, table, picked).astype(BF16)
    spread[...] = raw_ref[...].astype(F32).reshape(plan.raw * plan.windows, plan.channels)
    series = [
        spread[pl.ds(w, plan.raw, stride=plan.windows), :].astype(BF16) for w in range(plan.windows)
    ]
    rows = jnp.dot(table, jnp.concatenate(series, axis=1), preferred_element_type=F32).astype(BF16)
    out_ref[...] = rows
    kept_ref[0 : plan.rows, :] = rows
    both[...] = jnp.zeros((SUB, LANES), F32)
    both[0:1, 0 : plan.dec_taps] = taps_ref[...]
    both[1:2, 0 : plan.bp_taps] = bp_ref[...]
    kept_ref[plan.rows :, 0:LANES] = both[...].astype(BF16)


def local_rows(plan, raw, dec_taps, bp_taps):
    return pl.pallas_call(
        functools.partial(local_kernel, plan),
        out_shape=(
            jax.ShapeDtypeStruct((plan.rows, plan.wide), BF16),
            jax.ShapeDtypeStruct((plan.rows + SUB, plan.wide), BF16),
        ),
        in_specs=[VMEM, VMEM, VMEM],
        out_specs=(VMEM, VMEM),
        scratch_shapes=[
            pltpu.VMEM((plan.raw * plan.windows, plan.channels), F32),
            pltpu.VMEM((SUB, LANES), F32),
        ],
        name="local_rows",
    )(dec_taps, bp_taps, jnp.transpose(raw, (2, 0, 1)))


def table_kernel(plan, rows_ref, band_ref, edge_ref, kept_ref):
    kept_ref[...] = rows_ref[0 : plan.rows, :]
    dec_ref, bp_ref = (rows_ref[plan.rows :, 0:LANES].astype(F32)[k : k + 1] for k in range(2))
    span = ceil_to(plan.total + plan.bp_taps, LANES)
    lane = lax.broadcasted_iota(jnp.int32, (1, span), 1)
    base = jnp.zeros((1, span), F32)
    for k in range(plan.bp_taps):
        base = jnp.where(lane == (span - k) % span, rounded_tap(bp_ref, k), base)
    col = lax.broadcasted_iota(jnp.int32, (span, plan.joined), 1)
    time = lax.broadcasted_iota(jnp.int32, (span, plan.joined), 0)
    at = jnp.full((span, plan.joined), -1, jnp.int32)
    for p in range(plan.lag_total):
        start = col - p * plan.slot
        at = jnp.where((start >= 0) & (start < plan.whole), start + p * plan.dec + plan.head, at)
        start = col - plan.held - p * plan.head
        at = jnp.where((start >= 0) & (start < plan.head), start + p * plan.dec, at)
    order = jnp.where(time == at, 1.0, 0.0).astype(BF16)
    for parity in range(2):
        spread = jnp.broadcast_to(base, (plan.half, span))
        taps = pltpu.roll(spread, parity, 1, stride=2, stride_axis=0)
        band_ref[parity * plan.half : (parity + 1) * plan.half, :] = jnp.dot(taps.astype(BF16), order, preferred_element_type=F32).astype(BF16)
    rows = plan.joined - plan.held
    row = lax.broadcasted_iota(jnp.int32, (rows, plan.held), 0)
    col = lax.broadcasted_iota(jnp.int32, (rows, plan.held), 1)
    tap = jnp.full((rows, plan.held), -1, jnp.int32)
    for p in range(plan.lag_total):
        j = row - p * plan.head
        mine = (j >= 0) & (j < plan.head)
        r = col - p * plan.slot - plan.whole - plan.edge
        tap = jnp.where(mine & (r >= 0) & (r < plan.edge), 2 * j - r, tap)
        r = col - (p - 1) * plan.slot - plan.whole
        tap = jnp.where(mine & (r >= 0) & (r < plan.edge), 2 * j + plan.edge - r, tap)
    table = jnp.zeros((rows, plan.held), F32)
    for k in range(plan.dec_taps):
        table = jnp.where(tap == k, rounded_tap(dec_ref, k), table)
    edge_ref[...] = table.astype(BF16)


def tables(plan, rows):
    return pl.pallas_call(
        functools.partial(table_kernel, plan),
        out_shape=(
            jax.ShapeDtypeStruct((2 * plan.half, plan.joined), BF16),
            jax.ShapeDtypeStruct((plan.joined - plan.held, plan.held), BF16),
            jax.ShapeDtypeStruct((plan.rows, plan.wide), BF16),
        ),
        in_specs=[VMEM],
        out_specs=(VMEM, VMEM, VMEM),
        compiler_params=pltpu.CompilerParams(vmem_limit_bytes=12 * 2**20),
        cost_estimate=pl.CostEstimate(flops=500_000_000, bytes_accessed=2_000_000, transcendentals=0),
        name="tables",
    )(rows)


def make_series(plan, place_ref, pieces, tables_refs, held, even, odd, ahead, right):
    place = place_ref[0]
    if plan.slot > plan.rows:
        for p in range(plan.lag_total):
            held[(p + 1) * plan.slot - 16 : (p + 1) * plan.slot, :] = jnp.zeros((16, plan.wide), BF16)
    places = [
        pl.ds(pl.multiple_of(lax.bitwise_xor(place, p) * plan.slot, 16), plan.rows)
        for p in range(plan.lag_total)
    ]
    for p, piece in enumerate(pieces):
        held[places[p], :] = piece[...]
    for ref in (even, odd, ahead):
        ref[0 : plan.pad, :] = jnp.zeros((plan.pad, plan.wide), F32)
        ref[plan.pad + plan.half - SUB :, :] = jnp.zeros(
            (plan.padded - plan.pad - plan.half + SUB, plan.wide), F32
        )
    filter_block(plan, tables_refs, held, even, odd, ahead)
    lay_right(plan, place, even, odd, ahead, right)


def filter_block(plan, tables_refs, held, even, odd, ahead):
    band_ref, edge_ref = tables_refs
    held[plan.held : plan.joined, :] = jnp.dot(
        edge_ref[...], held[0 : plan.held, :], preferred_element_type=F32
    ).astype(BF16)
    step = 2 * LANES
    for c in range(0, plan.wide, step):
        cols = slice(c, c + step)
        block = held[:, cols]
        both = jnp.dot(band_ref[...], block, preferred_element_type=F32)
        a, b = both[0 : plan.half], both[plan.half :]
        power = jnp.sum(a * a + b * b, axis=0, keepdims=True) * (1.0 / plan.total)
        scale = lax.rsqrt(power + 1e-06)
        a = (a * scale).astype(BF16).astype(F32)
        b = (b * scale).astype(BF16).astype(F32)
        even[plan.pad : plan.pad + plan.half, cols] = a
        odd[plan.pad : plan.pad + plan.half, cols] = b
        ahead[plan.pad - 1 : plan.pad - 1 + plan.half, cols] = a


def lay_right(plan, place, even, odd, ahead, right):
    base = place * (plan.lags // 2)
    for w in range(plan.windows):
        cols = slice(w * plan.channels, (w + 1) * plan.channels)
        for first in range(2):
            at = pl.ds(pl.multiple_of(base + first * SUB, SUB), plan.pitch)
            a, b, c = even[at, cols], odd[at, cols], ahead[at, cols]
            to = slice(first * plan.channels, (first + 1) * plan.channels)
            for k, value in enumerate((b, a - b, c - b)):
                right[k, w * plan.pitch : (w + 1) * plan.pitch, to] = value.astype(BF16)


def right_operand(plan, k, n, right):
    def rows(k, low, high):
        parts = []
        for w in range(plan.windows):
            start, stop = max(low, w * plan.depth), min(high, (w + 1) * plan.depth)
            if start < stop:
                at = w * (plan.pitch - plan.depth) + 2 * SUB * n
                parts.append(right[k, at + start : at + stop, :])
        return parts

    if k == 0:
        return jnp.concatenate(rows(0, 0, plan.even), axis=0)
    return jnp.concatenate(rows(k, 0, plan.deep) + rows(0, plan.even, plan.deep), axis=0)


def make_left(plan, even, odd, stacks, mixes, left):
    for ref, stack in zip((even, odd), stacks, strict=True):
        stack[0:SUB, :] = jnp.zeros((SUB, plan.channels), F32)
        for w in range(plan.windows):
            stack[SUB + w * plan.depth : SUB + (w + 1) * plan.depth, :] = ref[
                plan.pad : plan.pad + plan.depth, w * plan.channels : (w + 1) * plan.channels
            ]
    for n, c in enumerate(range(0, plan.deep, LANES)):
        mixed = mixes[n % len(mixes)]
        for delay in range(SUB):
            rows = slice(SUB - delay + c, SUB - delay + c + LANES)
            for e, stack in enumerate(stacks):
                mixed[e, pl.ds(delay, plan.channels, stride=PITCH), :] = stack[rows, :].T
        for r in range(0, plan.channels * SUB, LANES):
            a, b = (
                jnp.concatenate(
                    [mixed[e, i * PITCH : i * PITCH + SUB, :] for i in range(r // SUB, (r + LANES) // SUB)], axis=0
                )
                for e in range(2)
            )
            for k, value in enumerate((a + b, a, b)):
                value = value.astype(BF16)
                if k > 0 or c < plan.even:
                    left[k, r : r + LANES, c : c + LANES] = value
                else:
                    for other in (1, 2):
                        at = c - plan.even + plan.deep
                        left[other, r : r + LANES, at : at + LANES] = value


def correlate(plan, count, left, right, out_ref):
    factor = 1.0 / math.sqrt(plan.windows * plan.total)
    for n in range(plan.shifts // 2):
        rows = pl.ds(pl.multiple_of(pl.program_id(0) * count * SUB, count * SUB), count * SUB)
        both, even, odd = (
            jnp.dot(left[k, rows, :deep], right_operand(plan, k, n, right), preferred_element_type=F32)
            for k, deep in enumerate((plan.even, plan.full, plan.full))
        )
        for parity, value in ((0, even), (1, odd)):
            value = (both + value) * factor
            for first in range(2):
                s = 2 * n + first
                part = value[:, first * plan.channels : (first + 1) * plan.channels]
                out_ref[:, 0, pl.ds(2 * SUB * s + parity, SUB, stride=2), :] = part.reshape(
                    count, SUB, plan.channels
                )


def own_kernel(plan, place_ref, *refs):
    n = plan.lag_total
    pieces, tabs, (left_ref, right_ref) = refs[:n], refs[n : n + 2], refs[n + 2 : n + 4]
    held, even, odd, ahead, *rest = refs[n + 4 :]
    make_series(plan, place_ref, pieces, tabs, held, even, odd, ahead, right_ref)
    make_left(plan, even, odd, rest[:2], rest[2:], left_ref)


def first_kernel(plan, count, left_ref, right_ref, out_ref):
    correlate(plan, count, left_ref, right_ref, out_ref)


def other_kernel(plan, count, place_ref, *refs):
    n = plan.lag_total
    pieces, tabs, left_ref, out_ref = refs[:n], refs[n : n + 2], refs[n + 2], refs[n + 4]
    held, even, odd, ahead, right = refs[n + 5 :]

    @pl.when(pl.program_id(0) == 0)
    def _():
        make_series(plan, place_ref, pieces, tabs, held, even, odd, ahead, right)

    correlate(plan, count, left_ref, right, out_ref)


def series_scratch(plan):
    return [pltpu.VMEM((plan.joined, plan.wide), BF16)] + [pltpu.VMEM((plan.padded, plan.wide), F32)] * 3


def prepare_own(plan, place, pieces, tabs):
    return pl.pallas_call(
        functools.partial(own_kernel, plan),
        out_shape=(
            jax.ShapeDtypeStruct((3, plan.channels * SUB, plan.full), BF16),
            jax.ShapeDtypeStruct((3, plan.windows * plan.pitch, 2 * plan.channels), BF16),
        ),
        in_specs=[SMEM] + [VMEM] * (plan.lag_total + 2),
        out_specs=(VMEM, VMEM),
        scratch_shapes=series_scratch(plan)
        + [pltpu.VMEM((SUB + plan.deep, plan.channels), F32)] * 2
        + [pltpu.VMEM((2, plan.channels * PITCH, LANES), F32)],
        compiler_params=pltpu.CompilerParams(vmem_limit_bytes=33 * 2**20),
        cost_estimate=pl.CostEstimate(flops=100_000_000, bytes_accessed=2**18, transcendentals=0),
        name="prepare_own",
    )(place, *pieces, *tabs)


def correlation_parts(plan, count, pairs, distance):
    out_shape = jax.ShapeDtypeStruct((plan.channels, pairs, plan.lags, plan.channels), F32)
    out_spec = pl.BlockSpec((count, 1, plan.lags, plan.channels), lambda i: (i, distance, 0, 0))
    flops = 2 * 3 * plan.channels * SUB * plan.deep * plan.shifts * plan.channels
    cost = pl.CostEstimate(flops=flops, bytes_accessed=8 * 2**20, transcendentals=0)
    return out_shape, out_spec, cost


def own_correlation(plan, count, pairs, left, right):
    out_shape, out_spec, cost = correlation_parts(plan, count, pairs, 0)
    return pl.pallas_call(
        functools.partial(first_kernel, plan, count),
        grid=(plan.channels // count,),
        out_shape=out_shape,
        in_specs=[VMEM, VMEM],
        out_specs=out_spec,
        compiler_params=pltpu.CompilerParams(vmem_limit_bytes=24 * 2**20),
        cost_estimate=cost,
        name="own_correlation",
    )(left, right)


def other_correlation(plan, count, pairs, distance, place, pieces, tabs, left, out):
    out_shape, out_spec, cost = correlation_parts(plan, count, pairs, distance)
    in_specs = [SMEM] + [VMEM] * (plan.lag_total + 3) + [pl.BlockSpec(memory_space=pl.ANY)]
    return pl.pallas_call(
        functools.partial(other_kernel, plan, count),
        grid=(plan.channels // count,),
        out_shape=out_shape,
        in_specs=in_specs,
        out_specs=out_spec,
        scratch_shapes=series_scratch(plan)
        + [pltpu.VMEM((3, plan.windows * plan.pitch, 2 * plan.channels), BF16)],
        input_output_aliases={len(in_specs) - 1: 0},
        compiler_params=pltpu.CompilerParams(vmem_limit_bytes=30 * 2**20),
        cost_estimate=cost,
        name="other_correlation",
    )(place, *pieces, *tabs, left, out)


def swap(piece, mask):
    count = lax.axis_size("lag")
    return lax.ppermute(piece, "lag", [(i ^ mask, i) for i in range(count)])


def from_ahead(piece, distance):
    count = lax.axis_size("chan")
    return lax.ppermute(piece, "chan", [((i + distance) % count, i) for i in range(count)])


def same_core(piece):
    return [swap(piece, mask) if mask else piece for mask in range(0, lax.axis_size("lag"), 2)]


def both_cores(held):
    return [x for piece in held for x in (piece, swap(piece, 1))]


def shards(raw_samples, decimation_taps, bandpass_taps):
    plan = Plan(raw_samples.shape, lax.axis_size("lag"), decimation_taps.shape[0], bandpass_taps.shape[0])
    pairs = lax.axis_size("chan") // 2 + 1
    place = lax.axis_index("lag").astype(jnp.int32).reshape(1)
    piece, kept = local_rows(
        plan, raw_samples, decimation_taps.reshape(1, -1), bandpass_taps.reshape(1, -1)
    )
    *tabs, kept = tables(plan, kept)
    count = 64
    own = same_core(piece)
    near = from_ahead(piece, 1)
    tabs, own[1:] = lax.optimization_barrier((tabs, own[1:]))
    pieces, near = lax.optimization_barrier((both_cores(own), near))
    left, right = prepare_own(plan, place, [kept, *pieces[1:]], tabs)
    left, near, piece = lax.optimization_barrier((left, near, piece))
    held = same_core(near)
    far = {distance: from_ahead(piece, distance) for distance in range(2, pairs)}
    out = own_correlation(plan, count, pairs, left, right)
    for distance in range(1, pairs):
        out, held, far = lax.optimization_barrier((out, held, far))
        pieces = both_cores(held)
        if distance + 1 < pairs:
            held = same_core(far[distance + 1])
        out = other_correlation(plan, count, pairs, distance, place, pieces, tabs, left, out)
    return out


def solution(mesh):
    placed = (P(None, "chan", "lag"), P(), P())
    return jax.shard_map(
        shards, mesh=mesh, in_specs=placed, out_specs=P("chan", None, "lag", None), check_vma=False
    )
```
